32 devices in a mesh: dp: 8 (over z, y), mp: 4 (over x, core).
Axes of the slice: x: 2, y: 2, z: 4, core: 2. Of those that a mesh axis runs over, the one named last changes fastest.
Arguments:
- tokens: bfloat16 [64, 8192], P('dp'), may hold values from -1000 to 1000
- norm_gain: float32 [8192], replicated, may hold values from 0.5 to 1.5
- target: bfloat16 [64, 8192], P(None, 'mp'), may hold values from -6 to 6
- w_gate: bfloat16 [8192, 24576], P('mp', 'dp'), may hold values from -0.0625 to 0.0625
- w_up: bfloat16 [8192, 24576], P('mp', 'dp'), may hold values from -0.0625 to 0.0625
- v_gate: bfloat16 [8192, 24576], P('mp', 'dp'), may hold values from -6 to 6
- w_down: bfloat16 [24576, 8192], P('dp', 'mp'), may hold values from -0.0390625 to 0.0390625
- v_down: bfloat16 [24576, 8192], P('dp', 'mp'), may hold values from -6 to 6
Outputs:
- gate_score: bfloat16 [8192, 24576], P('mp', 'dp')
- down_score: bfloat16 [24576, 8192], P('dp', 'mp')
The draws below stay inside these ranges and needn't reach their ends.
All inputs are finite; a program needn't handle non-finite values.
Results may differ from the reference program's by a relative error of at most 0.0083.
Values may be sent and summed in bfloat16 or wider, within the bound.
No kernel may reach another device: no remote copies, remote signals or barrier semaphores. Data moves between devices by JAX's collectives and lax.ppermute only.
A program may use at most 256 MiB of HBM per device.

```python
import math
import jax
import jax.numpy as jnp
from jax import lax

D = 8192
FF = 24576
TOKENS = 64


def draw_tokens(key, part):
    key = jax.random.fold_in(key, 11)
    key_base, key_row, key_col = jax.random.split(key, 3)
    position = jnp.arange(D, dtype=jnp.float32)[None, :] / D
    row_scale = jnp.exp(jax.random.uniform(key_row, (TOKENS, 1), jnp.float32, 0.0, math.log(10.0)))
    base_noise = jnp.clip(jax.random.normal(key_base, (TOKENS, D), jnp.float32), -6.0, 6.0)
    col_scale = jnp.exp(math.log(10.0) * position) * jnp.exp(jax.random.uniform(key_col, (1, D), jnp.float32, -0.35, 0.35))
    return (base_noise * row_scale * col_scale).astype(jnp.bfloat16)


def shard_levels(own_key, shape, pieces, least, top_value):
    def one(dim, shards_of):
        steps = jax.random.uniform(jax.random.fold_in(jax.random.fold_in(own_key, 6), dim), (shards_of,), jnp.float32, least / len(pieces), top_value / len(pieces))
        return jnp.repeat(jnp.exp(steps), shape[dim] // shards_of).reshape((-1,) + (1,) * (len(shape) - dim - 1))

    gain = one(*pieces[0])
    for cut in pieces[1:]:
        gain = gain * one(*cut)
    return gain


def bell_draw(stream_key, extent, width, most, cuts=(), kind=jnp.bfloat16):
    level = shard_levels(stream_key, extent, cuts, -0.22, 0.18) if cuts else 1.0
    array = jax.random.normal(stream_key, extent, jnp.float32) * width * level
    return jnp.minimum(jnp.maximum(array, -most), most).astype(kind)


def setup_inputs(seed: int = 0) -> dict:
    keys = jax.random.split(jax.random.key(seed), 9)
    tokens = draw_tokens(jax.random.fold_in(keys[8], 71), 0)
    norm_gain = jnp.clip(1.0 + 0.1 * jax.random.normal(keys[1], (D,), jnp.float32), 0.5, 1.5)
    target = bell_draw(keys[2], (TOKENS, D), 1.0, 6.0, ((1, 4),))
    w_gate = bell_draw(keys[3], (D, FF), D ** -0.5, 0.0625, ((0, 4), (1, 8)))
    w_up = bell_draw(keys[4], (D, FF), D ** -0.5, 0.0625, ((0, 4), (1, 8)))
    v_gate = bell_draw(keys[5], (D, FF), 1.0, 6.0, ((0, 4), (1, 8)))
    w_down = bell_draw(keys[6], (FF, D), FF ** -0.5, 0.0390625, ((0, 8), (1, 4)))
    v_down = bell_draw(keys[7], (FF, D), 1.0, 6.0, ((0, 8), (1, 4)))
    return {"tokens": tokens, "norm_gain": norm_gain, "target": target, "w_gate": w_gate, "w_up": w_up, "v_gate": v_gate, "w_down": w_down, "v_down": v_down}


epsilon = 1e-06

def contract_rows(left_op, right_op):
    return lax.dot_general(left_op, right_op, (((0,), (0,)), ((), ())), preferred_element_type=jnp.float32)

def contract_cols(left_op, right_op):
    return lax.dot_general(left_op, right_op, (((1,), (1,)), ((), ())), preferred_element_type=jnp.float32)

def silu_parts(gate_pre):
    sigmoid_gate = jax.nn.sigmoid(gate_pre)
    activation = gate_pre * sigmoid_gate
    slope_gate = sigmoid_gate * (1.0 + gate_pre * (1.0 - sigmoid_gate))
    curvature = sigmoid_gate * (1.0 - sigmoid_gate) * (2.0 + gate_pre * (1.0 - 2.0 * sigmoid_gate))
    return (activation, slope_gate, curvature)

def reference(tokens, norm_gain, target, w_gate, w_up, v_gate, w_down, v_down):
    tokens_f = tokens.astype(jnp.float32)
    squares = lax.optimization_barrier(jnp.sum(tokens_f * tokens_f, axis=1, keepdims=True))
    normed = (tokens_f * lax.rsqrt(squares / tokens.shape[1] + epsilon) * norm_gain).astype(jnp.bfloat16)
    gate_pre = jnp.dot(normed, w_gate, preferred_element_type=jnp.float32)
    up_value = jnp.dot(normed, w_up, preferred_element_type=jnp.float32)
    tangent = jnp.dot(normed, v_gate, preferred_element_type=jnp.float32)
    activation, slope_gate, curvature = silu_parts(gate_pre)
    hidden = (activation * up_value).astype(jnp.bfloat16)
    hidden_tan = (slope_gate * up_value * tangent).astype(jnp.bfloat16)
    output = jnp.dot(hidden, w_down, preferred_element_type=jnp.float32)
    output_tan = jnp.dot(hidden_tan, w_down, preferred_element_type=jnp.float32) + jnp.dot(hidden, v_down, preferred_element_type=jnp.float32)
    token_count = tokens.shape[0]
    residual = ((output - target.astype(jnp.float32)) / token_count).astype(jnp.bfloat16)
    residual_tan = (output_tan / token_count).astype(jnp.bfloat16)
    down_hess = contract_rows(hidden_tan, residual) + contract_rows(hidden, residual_tan)
    back_grad = contract_cols(residual, w_down)
    back_tangent = contract_cols(residual_tan, w_down) + contract_cols(residual, v_down)
    combined = (back_tangent * up_value * slope_gate + back_grad * up_value * curvature * tangent).astype(jnp.bfloat16)
    gate_hess = contract_rows(normed, combined)
    gate_score = (v_gate.astype(jnp.float32) * gate_hess).astype(jnp.bfloat16)
    down_score = (v_down.astype(jnp.float32) * down_hess).astype(jnp.bfloat16)
    return (gate_score, down_score)
```

```python
import jax
import jax.numpy as jnp
from jax import lax
from jax.sharding import PartitionSpec as P

epsilon = 1e-06
bf16 = jnp.bfloat16
f32 = jnp.float32


def contract_rows(left_op, right_op):
    return lax.dot_general(
        left_op, right_op, (((0,), (0,)), ((), ())), preferred_element_type=f32
    )


def contract_cols(left_op, right_op):
    return lax.dot_general(
        left_op, right_op, (((1,), (1,)), ((), ())), preferred_element_type=f32
    )


def silu_parts(gate_pre):
    sigmoid_gate = jax.nn.sigmoid(gate_pre)
    activation = gate_pre * sigmoid_gate
    slope_gate = sigmoid_gate * (1.0 + gate_pre * (1.0 - sigmoid_gate))
    curvature = sigmoid_gate * (1.0 - sigmoid_gate) * (2.0 + gate_pre * (1.0 - 2.0 * sigmoid_gate))
    return (activation, slope_gate, curvature)


def swap_core(value):
    return lax.ppermute(value, "mp", [(i, i ^ 1) for i in range(4)])


def swap_chip(value):
    return lax.ppermute(value, "mp", [(i, i ^ 2) for i in range(4)])


def reduce_mp(parts, core):
    half = parts.shape[1] // 2
    keep = lax.dynamic_slice_in_dim(parts, core * half, half, 1)
    send = lax.dynamic_slice_in_dim(parts, (1 - core) * half, half, 1).astype(bf16)
    chip_sum = keep + swap_core(send).astype(f32)
    return chip_sum + swap_chip(chip_sum.astype(bf16)).astype(f32)


def gather_core(mine, core):
    other = swap_core(mine)
    low = jnp.where(core == 0, mine, other)
    high = jnp.where(core == 0, other, mine)
    return jnp.concatenate([low, high], axis=1)


def gather_dp(block, dp):
    copies = jnp.broadcast_to(block[None], (dp,) + block.shape)
    return lax.all_to_all(copies, "dp", 0, 0, tiled=True)


def per_device(dp, tokens, norm_gain, target, w_gate, w_up, v_gate, w_down, v_down):
    feature_count = tokens.shape[1]
    own = tokens.shape[0]
    token_count = own * dp
    col_width = w_gate.shape[0]
    mp_id = lax.axis_index("mp")
    dp_id = lax.axis_index("dp")
    core = mp_id % 2
    col_first = mp_id * col_width
    tokens_f = tokens.astype(f32)
    squares = jnp.sum(tokens_f * tokens_f, axis=1, keepdims=True)
    normed_rows = (tokens_f * lax.rsqrt(squares / feature_count + epsilon) * norm_gain).astype(bf16)
    local_cols = lax.dynamic_slice_in_dim(normed_rows, col_first, col_width, 1)
    normed = gather_dp(local_cols, dp).reshape(token_count, col_width)
    gate_part = jnp.dot(normed, w_gate, preferred_element_type=f32)
    up_part = jnp.dot(normed, w_up, preferred_element_type=f32)
    tangent_part = jnp.dot(normed, v_gate, preferred_element_type=f32)
    gate_pre, up_value, tangent = reduce_mp(jnp.stack([gate_part, up_part, tangent_part]), core)
    activation, slope_gate, curvature = silu_parts(gate_pre)
    hidden_half = (activation * up_value).astype(bf16)
    hidden_tan_half = (slope_gate * up_value * tangent).astype(bf16)
    both = gather_core(jnp.stack([hidden_half, hidden_tan_half]), core)
    hidden, hidden_tan = both[0], both[1]
    out_part = jnp.dot(hidden, w_down, preferred_element_type=f32)
    out_tan_part = jnp.dot(hidden_tan, w_down, preferred_element_type=f32) + jnp.dot(
        hidden, v_down, preferred_element_type=f32
    )
    pieces = jnp.stack(
        [out_part.reshape(dp, own, col_width), out_tan_part.reshape(dp, own, col_width)], axis=1
    ).astype(bf16)
    arrived = lax.all_to_all(pieces, "dp", 0, 0, tiled=True).astype(f32)
    totals = jnp.sum(arrived, axis=0)
    target_rows = lax.dynamic_slice_in_dim(target, dp_id * own, own, 0)
    residual_rows = ((totals[0] - target_rows.astype(f32)) / token_count).astype(bf16)
    residual_tan_rows = (totals[1] / token_count).astype(bf16)
    spread = gather_dp(jnp.stack([residual_rows, residual_tan_rows]), dp)
    residual = spread[:, 0].reshape(token_count, col_width)
    residual_tan = spread[:, 1].reshape(token_count, col_width)
    back_part = contract_cols(residual, w_down)
    back_tan_part = contract_cols(residual_tan, w_down) + contract_cols(residual, v_down)
    back_grad, back_tangent = reduce_mp(jnp.stack([back_part, back_tan_part]), core)
    down_hess = contract_rows(hidden_tan, residual) + contract_rows(hidden, residual_tan)
    down_score = (v_down.astype(f32) * down_hess).astype(bf16)
    combined_half = (
        back_tangent * up_value * slope_gate + back_grad * up_value * curvature * tangent
    ).astype(bf16)
    combined = gather_core(combined_half[None], core)[0]
    gate_hess = contract_rows(normed, combined)
    gate_score = (v_gate.astype(f32) * gate_hess).astype(bf16)
    return (gate_score, down_score)


def solution(mesh):
    dp = mesh.shape["dp"]
    in_specs = (
        P("dp", None),
        P(),
        P(None, "mp"),
        P("mp", "dp"),
        P("mp", "dp"),
        P("mp", "dp"),
        P("dp", "mp"),
        P("dp", "mp"),
    )
    out_specs = (P("mp", "dp"), P("dp", "mp"))

    def body(*args):
        return per_device(dp, *args)

    return jax.shard_map(body, mesh=mesh, in_specs=in_specs, out_specs=out_specs, check_vma=False)
```

```python
import functools
import jax
import jax.numpy as jnp
from jax import lax
from jax.experimental import pallas as pl
from jax.experimental.pallas import tpu as pltpu
from jax.sharding import PartitionSpec as P

epsilon = 1e-06
bf16 = jnp.bfloat16
f32 = jnp.float32
MIB = 1024 * 1024
IN_VMEM = pl.BlockSpec(memory_space=pltpu.VMEM)
IN_HBM = pl.BlockSpec(memory_space=pltpu.HBM)


def block_of(extent, most):
    size = most
    while extent % size:
        size -= 128
    return size


def params(mebibytes):
    return pltpu.CompilerParams(vmem_limit_bytes=mebibytes * MIB)


def cost(flops, bytes_accessed):
    return pl.CostEstimate(flops=flops, bytes_accessed=bytes_accessed, transcendentals=0)


def dot(left, right, left_dim, right_dim):
    return lax.dot_general(
        left, right, (((left_dim,), (right_dim,)), ((), ())), preferred_element_type=f32
    )


def held(value):
    return pltpu.with_memory_space_constraint(value, pltpu.VMEM)


def kept_out(value):
    return pltpu.with_memory_space_constraint(value, pltpu.HBM)


def silu_parts(gate_pre):
    sigmoid_gate = jax.nn.sigmoid(gate_pre)
    activation = gate_pre * sigmoid_gate
    slope_gate = sigmoid_gate * (1.0 + gate_pre * (1.0 - sigmoid_gate))
    curvature = sigmoid_gate * (1.0 - sigmoid_gate) * (2.0 + gate_pre * (1.0 - 2.0 * sigmoid_gate))
    return (activation, slope_gate, curvature)


def swap_core(value):
    return lax.ppermute(value, "mp", [(i, i ^ 1) for i in range(4)])


def swap_chip(value):
    return lax.ppermute(value, "mp", [(i, i ^ 2) for i in range(4)])


def load_call(weights, after, name):
    n = len(weights)
    parts = 4

    def body(*refs):
        sources, targets, sems = refs[:n], refs[n + 1 : 2 * n + 1], refs[-1]
        copies = []
        for i in range(n):
            rows = sources[i].shape[0] // parts
            for j in range(parts):
                span = pl.ds(j * rows, rows)
                copies.append(
                    pltpu.make_async_copy(
                        sources[i].at[span], targets[i].at[span], sems.at[i, j]
                    )
                )
        for copy in copies:
            copy.start()
        for copy in copies:
            copy.wait()

    size = sum(w.size * 2 for w in weights)
    return pl.pallas_call(
        body,
        in_specs=[IN_HBM] * n + [pl.BlockSpec(memory_space=pl.ANY)],
        out_specs=[IN_VMEM] * n,
        out_shape=[pltpu.VMEM(w.shape, w.dtype) for w in weights],
        scratch_shapes=[pltpu.SemaphoreType.DMA((n, parts))],
        compiler_params=params(1),
        cost_estimate=cost(0, 2 * size),
        name=name,
    )(*[kept_out(w) for w in weights], after)


def norm_call(tokens, norm_gain, copies, col_width):
    own, features = tokens.shape

    def body(tokens_ref, gain_ref, out_ref, scaled):
        tokens_f = tokens_ref[...].astype(f32)
        squares = jnp.sum(tokens_f * tokens_f, axis=1, keepdims=True)
        scaled[...] = tokens_f * lax.rsqrt(squares / features + epsilon) * gain_ref[...]
        first = pl.multiple_of(lax.axis_index("mp") * col_width, col_width)
        mine = scaled[:, pl.ds(first, col_width)].astype(bf16)
        for i in range(copies):
            out_ref[i] = mine

    return pl.pallas_call(
        body,
        out_shape=jax.ShapeDtypeStruct((copies, own, col_width), bf16),
        scratch_shapes=[pltpu.VMEM((own, features), f32)],
        compiler_params=params(8),
        name="norm_rows",
    )(tokens, norm_gain.reshape(1, features))


def gate_call(normed, w_gate, w_up, v_gate, chunk, chunks):
    count, depth = normed.shape
    half = count // 2
    width = w_gate.shape[1] // chunks
    block = block_of(width, 256)
    first = chunk * (width // block)

    def body(normed_ref, gate_ref, up_ref, tan_ref, keep_ref, send_ref):
        upper = lax.axis_index("mp") % 2 == 1
        for i, weight in enumerate((gate_ref, up_ref, tan_ref)):
            part = dot(normed_ref[...], weight[...], 1, 0)
            low, high = part[:half], part[half:]
            keep_ref[i] = jnp.where(upper, high, low)
            send_ref[i] = jnp.where(upper, low, high).astype(bf16)

    weight_spec = pl.BlockSpec((depth, block), lambda i: (0, first + i))
    part_spec = pl.BlockSpec((3, half, block), lambda i: (0, 0, i))
    return pl.pallas_call(
        body,
        grid=(width // block,),
        in_specs=[pl.BlockSpec((count, depth), lambda i: (0, 0)), weight_spec, weight_spec, weight_spec],
        out_specs=[part_spec, part_spec],
        out_shape=[
            jax.ShapeDtypeStruct((3, half, width), f32),
            jax.ShapeDtypeStruct((3, half, width), bf16),
        ],
        compiler_params=params(20),
        cost_estimate=cost(6 * count * depth * width, 6 * depth * width),
        name="gate_products",
    )(normed, *[kept_out(w) for w in (w_gate, w_up, v_gate)])


def hidden_call(chip_sum, arrived, after):
    shape = chip_sum.shape[1:]
    width = shape[1]
    block = block_of(width, 512)

    def body(sum_ref, arrived_ref, after_ref, mine_ref, factor_ref):
        for j in range(width // block):
            span = slice(j * block, (j + 1) * block)
            gate_pre, up_value, tangent = [
                sum_ref[i, :, span] + arrived_ref[i, :, span].astype(f32) for i in range(3)
            ]
            activation, slope_gate, curvature = silu_parts(gate_pre)
            mine_ref[0, :, span] = (activation * up_value).astype(bf16)
            mine_ref[1, :, span] = (slope_gate * up_value * tangent).astype(bf16)
            factor_ref[0, :, span] = up_value * slope_gate
            factor_ref[1, :, span] = up_value * curvature * tangent

    return pl.pallas_call(
        body,
        in_specs=[IN_VMEM, IN_VMEM, pl.BlockSpec(memory_space=pl.ANY)],
        out_specs=[IN_VMEM] * 2,
        out_shape=[
            jax.ShapeDtypeStruct((2,) + shape, bf16),
            jax.ShapeDtypeStruct((2,) + shape, f32),
        ],
        compiler_params=params(8),
        cost_estimate=cost(0, 30 * shape[0] * width),
        name="hidden_units",
    )(chip_sum, arrived, after)


def down_call(mine, other, w_down, v_down):
    half, rows = mine.shape[1:]
    count = 2 * half
    features = w_down.shape[1]
    block = block_of(features, 512)

    def body(mine_ref, other_ref, w_ref, v_ref, out_ref, left):
        for i in range(2):
            left[i * count : i * count + half] = mine_ref[i]
            left[i * count + half : (i + 1) * count] = other_ref[i]
        for j in range(features // block):
            span = slice(j * block, (j + 1) * block)
            both = dot(left[...], w_ref[:, span], 1, 0)
            out_ref[0, :, span] = both[:count].astype(bf16)
            out_ref[1, :, span] = (both[count:] + dot(left[:count], v_ref[:, span], 1, 0)).astype(bf16)

    return pl.pallas_call(
        body,
        in_specs=[IN_VMEM] * 4,
        out_specs=IN_VMEM,
        out_shape=jax.ShapeDtypeStruct((2, count, features), bf16),
        scratch_shapes=[pltpu.VMEM((2 * count, rows), bf16)],
        compiler_params=params(12),
        cost_estimate=cost(6 * count * rows * features, 4 * rows * features),
        name="down_products",
    )(mine, other, held(w_down), held(v_down))


def back_call(residuals, w_down, v_down):
    count, features = residuals.shape[1:]
    half = count // 2
    rows = w_down.shape[0]
    block = block_of(rows, 512)

    def body(res_ref, w_ref, v_ref, keep_ref, send_ref, right):
        right[...] = res_ref[...].reshape(2 * count, features).T
        for j in range(rows // block):
            span = slice(j * block, (j + 1) * block)
            both = dot(w_ref[span, :], right[...], 1, 0)
            tangent = both[:, count:] + dot(v_ref[span, :], right[:, :count], 1, 0)
            for i, part in enumerate((both[:, :count].T, tangent.T)):
                keep_ref[i, :, span] = part[:half]
                send_ref[i, :, span] = part[half:].astype(bf16)

    return pl.pallas_call(
        body,
        in_specs=[IN_VMEM] * 3,
        out_specs=[IN_VMEM] * 2,
        out_shape=[
            jax.ShapeDtypeStruct((2, half, rows), f32),
            jax.ShapeDtypeStruct((2, half, rows), bf16),
        ],
        scratch_shapes=[pltpu.VMEM((features, 2 * count), bf16)],
        compiler_params=params(12),
        cost_estimate=cost(6 * count * rows * features, 4 * rows * features),
        name="back_products",
    )(residuals, held(w_down), held(v_down))


def down_score_call(mine, other, residuals, v_down):
    half, rows = mine.shape[1:]
    count = 2 * half
    features = v_down.shape[1]
    block = block_of(rows, 512)
    steps = rows // block

    def body(mine_ref, other_ref, res_ref, v_ref, out_ref, buffer, sems):
        copies = []
        for j in range(steps):
            span = slice(j * block, (j + 1) * block)
            if j >= 2:
                copies[j - 2].wait()
            left = jnp.concatenate(
                [mine_ref[1, :, span], other_ref[1, :, span], mine_ref[0, :, span], other_ref[0, :, span]],
                axis=0,
            )
            hess = dot(left, res_ref[...].reshape(2 * count, features), 0, 0)
            buffer[j % 2] = (v_ref[span, :].astype(f32) * hess).astype(bf16)
            copies.append(
                pltpu.make_async_copy(
                    buffer.at[j % 2], out_ref.at[pl.ds(j * block, block)], sems.at[j % 2]
                )
            )
            copies[j].start()
        for copy in copies[-2:]:
            copy.wait()

    return pl.pallas_call(
        body,
        in_specs=[IN_VMEM] * 4,
        out_specs=IN_HBM,
        out_shape=jax.ShapeDtypeStruct((rows, features), bf16),
        scratch_shapes=[
            pltpu.VMEM((2, block, features), bf16),
            pltpu.SemaphoreType.DMA((2,)),
        ],
        compiler_params=params(16),
        cost_estimate=cost(4 * count * rows * features, 4 * rows * features),
        name="down_score",
    )(mine, other, residuals, held(v_down))


def combine_call(chip_sum, arrived, factors, after):
    half, width = chip_sum.shape[1:]
    block = block_of(width, 512)

    def body(sum_ref, arrived_ref, factor_ref, after_ref, out_ref):
        for j in range(width // block):
            span = slice(j * block, (j + 1) * block)
            back_grad, back_tangent = [
                sum_ref[i, :, span] + arrived_ref[i, :, span].astype(f32) for i in range(2)
            ]
            out_ref[:, span] = (
                back_tangent * factor_ref[0, :, span] + back_grad * factor_ref[1, :, span]
            ).astype(bf16)

    return pl.pallas_call(
        body,
        in_specs=[IN_VMEM] * 3 + [pl.BlockSpec(memory_space=pl.ANY)],
        out_specs=IN_VMEM,
        out_shape=jax.ShapeDtypeStruct((half, width), bf16),
        compiler_params=params(8),
        cost_estimate=cost(0, 22 * half * width),
        name="combined",
    )(chip_sum, arrived, factors, after)


def gate_score_call(normed, mine, other, v_gate):
    count, depth = normed.shape
    half = count // 2
    width = v_gate.shape[1]
    block = block_of(width, 512)
    steps = width // block

    def body(normed_ref, mine_ref, other_ref, v_ref, out_ref, buffer, sems):
        upper = lax.axis_index("mp") % 2 == 1
        copies = []
        for j in range(steps):
            span = slice(j * block, (j + 1) * block)
            if j >= 2:
                copies[j - 2].wait()
            low = jnp.where(upper, other_ref[:, span], mine_ref[:, span])
            high = jnp.where(upper, mine_ref[:, span], other_ref[:, span])
            hess = dot(normed_ref[...], jnp.concatenate([low, high], axis=0), 0, 0)
            buffer[j % 2] = (v_ref[:, span].astype(f32) * hess).astype(bf16)
            copies.append(
                pltpu.make_async_copy(
                    buffer.at[j % 2], out_ref.at[:, pl.ds(j * block, block)], sems.at[j % 2]
                )
            )
            copies[j].start()
        for copy in copies[-2:]:
            copy.wait()

    return pl.pallas_call(
        body,
        in_specs=[IN_VMEM] * 4,
        out_specs=IN_HBM,
        out_shape=jax.ShapeDtypeStruct((depth, width), bf16),
        scratch_shapes=[
            pltpu.VMEM((2, depth, block), bf16),
            pltpu.SemaphoreType.DMA((2,)),
        ],
        compiler_params=params(16),
        cost_estimate=cost(2 * count * depth * width, 4 * depth * width),
        name="gate_score",
    )(normed, mine, other, v_gate)


def bits():
    index = lax.axis_index("dp")
    return index % 2, (index // 2) % 2


def swap_dp(value, bit):
    return lax.ppermute(value, "dp", [(i, i ^ bit) for i in range(8)])


def piece_call(mine, other, w_down, v_down, away, dtype):
    half, rows = mine.shape[1:]
    count = 2 * half
    features = w_down.shape[1]
    piece = features // 8

    def body(mine_ref, other_ref, w_ref, v_ref, a_ref, b_ref, left):
        y, z = bits()
        for i in range(2):
            left[i * count : i * count + half] = mine_ref[i]
            left[i * count + half : (i + 1) * count] = other_ref[i]
        for out_ref, base, outer, inner in ((a_ref, 0, y, z), (b_ref, 4, z, y)):
            group = 1 - outer if away else outer
            for k, low in enumerate((1 - inner, inner)):
                first = pl.multiple_of((base + 2 * group + low) * piece, piece)
                both = dot(left[...], w_ref[:, pl.ds(first, piece)], 1, 0)
                tangent = both[count:] + dot(left[:count], v_ref[:, pl.ds(first, piece)], 1, 0)
                out_ref[k, 0] = both[:count].astype(dtype)
                out_ref[k, 1] = tangent.astype(dtype)

    shape = jax.ShapeDtypeStruct((2, 2, count, piece), dtype)
    return pl.pallas_call(
        body,
        in_specs=[IN_VMEM] * 4,
        out_specs=[IN_VMEM] * 2,
        out_shape=[shape, shape],
        scratch_shapes=[pltpu.VMEM((2 * count, rows), bf16)],
        compiler_params=params(8),
        cost_estimate=cost(3 * count * rows * features, 2 * rows * features),
        name="pieces_away" if away else "pieces_home",
    )(mine, other, held(w_down), held(v_down))


def residual_call(sums, arrived, target):
    count, features = target.shape
    half = count // 2
    piece = features // 8

    def body(sums_ref, arrived_ref, target_ref, a_ref, b_ref):
        y, z = bits()
        upper = lax.axis_index("mp") % 2 == 1
        for i, (out_ref, outer, inner) in enumerate(((a_ref, y, z), (b_ref, z, y))):
            first = pl.multiple_of((4 * i + 2 * outer + inner) * piece, piece)
            wanted = target_ref[:, pl.ds(first, piece)].astype(f32)
            low, high = wanted[:half], wanted[half:]
            wanted = jnp.concatenate(
                [jnp.where(upper, high, low), jnp.where(upper, low, high)], axis=0
            )
            out_ref[0] = ((sums_ref[i, 0] + arrived_ref[i, 0].astype(f32) - wanted) / count).astype(bf16)
            out_ref[1] = ((sums_ref[i, 1] + arrived_ref[i, 1].astype(f32)) / count).astype(bf16)

    shape = jax.ShapeDtypeStruct((2, count, piece), bf16)
    return pl.pallas_call(
        body,
        in_specs=[IN_VMEM] * 3,
        out_specs=[IN_VMEM] * 2,
        out_shape=[shape, shape],
        compiler_params=params(4),
        cost_estimate=cost(0, 8 * 2 * count * piece),
        name="residuals",
    )(sums, arrived, target)


def back_first_call(a_pieces, b_pieces, w_down, v_down):
    count, piece = a_pieces.shape[2:]
    rows = w_down.shape[0]
    block = block_of(rows, 512)

    def body(a_ref, b_ref, w_ref, v_ref, out_ref, right):
        y, z = bits()
        for i, (ref, inner) in enumerate(((a_ref, z), (b_ref, y))):
            for k, low in enumerate((inner, 1 - inner)):
                first = pl.multiple_of((2 * i + low) * piece, piece)
                right[pl.ds(first, piece), :] = ref[k].reshape(2 * count, piece).T
        starts = [
            pl.multiple_of(2 * piece * y, 2 * piece),
            pl.multiple_of(2 * piece * (2 + z), 2 * piece),
        ]
        for j in range(rows // block):
            span = slice(j * block, (j + 1) * block)
            total = jnp.zeros((block, 2 * count), f32)
            tangent = jnp.zeros((block, count), f32)
            for i, first in enumerate(starts):
                part = right[2 * i * piece : 2 * (i + 1) * piece]
                total += dot(w_ref[span, pl.ds(first, 2 * piece)], part, 1, 0)
                tangent += dot(v_ref[span, pl.ds(first, 2 * piece)], part[:, :count], 1, 0)
            out_ref[span] = jnp.concatenate([total[:, :count], total[:, count:] + tangent], axis=1)

    return pl.pallas_call(
        body,
        in_specs=[IN_VMEM] * 4,
        out_specs=IN_VMEM,
        out_shape=jax.ShapeDtypeStruct((rows, 2 * count), f32),
        scratch_shapes=[pltpu.VMEM((4 * piece, 2 * count), bf16)],
        compiler_params=params(8),
        cost_estimate=cost(12 * count * rows * piece, 8 * rows * piece),
        name="back_first",
    )(a_pieces, b_pieces, held(w_down), held(v_down))


def back_second_call(a_pieces, b_pieces, a_far, b_far, first_part, w_down, v_down):
    count, piece = a_pieces.shape[2:]
    half = count // 2
    rows, features = w_down.shape
    block = block_of(rows, 512)

    def body(a_ref, b_ref, a_far_ref, b_far_ref, part_ref, w_ref, v_ref, keep_ref, send_ref, res_ref, right):
        y, z = bits()
        for i, (ref, far_ref, outer, inner) in enumerate(((a_ref, a_far_ref, y, z), (b_ref, b_far_ref, z, y))):
            for k, low in enumerate((inner, 1 - inner)):
                first = pl.multiple_of((2 * i + low) * piece, piece)
                right[pl.ds(first, piece), :] = far_ref[k].reshape(2 * count, piece).T
                near = pl.multiple_of((4 * i + 2 * outer + low) * piece, piece)
                far = pl.multiple_of((4 * i + 2 * (1 - outer) + low) * piece, piece)
                for t in range(2):
                    res_ref[t, :, pl.ds(near, piece)] = ref[k, t]
                    res_ref[t, :, pl.ds(far, piece)] = far_ref[k, t]
        starts = [
            pl.multiple_of(2 * piece * (1 - y), 2 * piece),
            pl.multiple_of(2 * piece * (3 - z), 2 * piece),
        ]
        for j in range(rows // block):
            span = slice(j * block, (j + 1) * block)
            total = part_ref[span]
            tangent = jnp.zeros((block, count), f32)
            for i, first in enumerate(starts):
                part = right[2 * i * piece : 2 * (i + 1) * piece]
                total += dot(w_ref[span, pl.ds(first, 2 * piece)], part, 1, 0)
                tangent += dot(v_ref[span, pl.ds(first, 2 * piece)], part[:, :count], 1, 0)
            for i, value in enumerate((total[:, :count].T, (total[:, count:] + tangent).T)):
                keep_ref[i, :, span] = value[:half]
                send_ref[i, :, span] = value[half:].astype(bf16)

    return pl.pallas_call(
        body,
        in_specs=[IN_VMEM] * 7,
        out_specs=[IN_VMEM] * 3,
        out_shape=[
            jax.ShapeDtypeStruct((2, half, rows), f32),
            jax.ShapeDtypeStruct((2, half, rows), bf16),
            jax.ShapeDtypeStruct((2, count, features), bf16),
        ],
        scratch_shapes=[pltpu.VMEM((4 * piece, 2 * count), bf16)],
        compiler_params=params(8),
        cost_estimate=cost(12 * count * rows * piece, 8 * rows * piece),
        name="back_second",
    )(a_pieces, b_pieces, a_far, b_far, first_part, held(w_down), held(v_down))


def middle_tree(mine, other, target, w_down, v_down):
    a_send, b_send = piece_call(mine, other, w_down, v_down, True, bf16)
    a_recv, b_recv = swap_dp(a_send, 1), swap_dp(b_send, 2)
    a_home, b_home = piece_call(mine, other, w_down, v_down, False, f32)
    a_sum = a_home + a_recv.astype(f32)
    b_sum = b_home + b_recv.astype(f32)
    a_recv, b_recv = swap_dp(a_sum[0].astype(bf16), 2), swap_dp(b_sum[0].astype(bf16), 1)
    sums = jnp.stack([a_sum[1] + a_recv.astype(f32), b_sum[1] + b_recv.astype(f32)])
    arrived = swap_dp(sums.astype(bf16), 4)
    a_res, b_res = residual_call(sums, arrived, target)
    a_pieces = jnp.stack([a_res, swap_dp(a_res, 2)])
    b_pieces = jnp.stack([b_res, swap_dp(b_res, 1)])
    a_far, b_far = swap_dp(a_pieces, 1), swap_dp(b_pieces, 2)
    first_part = back_first_call(a_pieces, b_pieces, w_down, v_down)
    return back_second_call(a_pieces, b_pieces, a_far, b_far, first_part, w_down, v_down)


def middle_direct(dp, mine, other, target, w_down, v_down):
    half = mine.shape[1]
    count = 2 * half
    own = count // dp
    features = w_down.shape[1]
    out_parts = down_call(mine, other, w_down, v_down)
    pieces = out_parts.reshape(2, dp, own, features).swapaxes(0, 1)
    arrived = lax.all_to_all(pieces, "dp", 0, 0, tiled=True).astype(f32)
    totals = jnp.sum(arrived, axis=0)
    core = lax.axis_index("mp") % 2
    first_row = (lax.axis_index("dp") * own + core * half) % count
    target_rows = lax.dynamic_slice_in_dim(target, first_row, own, 0)
    residual_rows = ((totals[0] - target_rows.astype(f32)) / count).astype(bf16)
    residual_tan_rows = (totals[1] / count).astype(bf16)
    rows = jnp.stack([residual_rows, residual_tan_rows])
    spread = lax.all_to_all(
        jnp.broadcast_to(rows[None], (dp,) + rows.shape), "dp", 0, 0, tiled=True
    )
    residuals = spread.swapaxes(0, 1).reshape(2, count, features)
    keep, send = back_call(residuals, w_down, v_down)
    return keep, send, residuals


def per_device(dp, tokens, norm_gain, target, w_gate, w_up, v_gate, w_down, v_down):
    own = tokens.shape[0]
    count = own * dp
    col_width = w_gate.shape[0]
    copies = norm_call(tokens, norm_gain, dp, col_width)
    normed = lax.all_to_all(copies, "dp", 0, 0, tiled=True).reshape(count, col_width)
    keep, send = gate_call(normed, w_gate, w_up, v_gate, 0, 1)
    chip_sum = keep + swap_core(send).astype(f32)
    chip_send = chip_sum.astype(bf16)
    w_down, v_down = load_call([w_down, v_down], chip_send, "load_down")
    mine, factors = hidden_call(chip_sum, swap_chip(chip_send), held(v_down))
    other = swap_core(mine)
    if dp == 8:
        keep, send, residuals = middle_tree(mine, other, target, w_down, v_down)
    else:
        keep, send, residuals = middle_direct(dp, mine, other, target, w_down, v_down)
    chip_sum = keep + swap_core(send).astype(f32)
    arrived = swap_chip(chip_sum.astype(bf16))
    down_score = down_score_call(mine, other, residuals, v_down)
    combined = combine_call(chip_sum, arrived, factors, down_score)
    gate_score = gate_score_call(normed, combined, swap_core(combined), v_gate)
    return (gate_score, down_score)


def solution(mesh):
    in_specs = (
        P("dp", None),
        P(),
        P(None, "mp"),
        P("mp", "dp"),
        P("mp", "dp"),
        P("mp", "dp"),
        P("dp", "mp"),
        P("dp", "mp"),
    )
    out_specs = (P("mp", "dp"), P("dp", "mp"))
    return jax.shard_map(
        functools.partial(per_device, mesh.shape["dp"]),
        mesh=mesh,
        in_specs=in_specs,
        out_specs=out_specs,
        check_vma=False,
    )
```

```python
import functools
import jax
import jax.numpy as jnp
from jax import lax
from jax.experimental import pallas as pl
from jax.experimental.pallas import tpu as pltpu
from jax.sharding import PartitionSpec as P

epsilon = 1e-06
bf16 = jnp.bfloat16
f32 = jnp.float32
MIB = 1024 * 1024
WAIT_FLOPS = 6 * 10**9
IN_VMEM = pl.BlockSpec(memory_space=pltpu.VMEM)
IN_HBM = pl.BlockSpec(memory_space=pltpu.HBM)


def block_of(extent, most):
    size = most
    while extent % size:
        size -= 128
    return size


def params(mebibytes):
    return pltpu.CompilerParams(vmem_limit_bytes=mebibytes * MIB)


def cost(flops, bytes_accessed):
    return pl.CostEstimate(flops=flops, bytes_accessed=bytes_accessed, transcendentals=0)


def dot(left, right, left_dim, right_dim):
    return lax.dot_general(
        left, right, (((left_dim,), (right_dim,)), ((), ())), preferred_element_type=f32
    )


def held(value):
    return pltpu.with_memory_space_constraint(value, pltpu.VMEM)


def kept_out(value):
    return pltpu.with_memory_space_constraint(value, pltpu.HBM)


def silu_parts(gate_pre):
    sigmoid_gate = jax.nn.sigmoid(gate_pre)
    activation = gate_pre * sigmoid_gate
    slope_gate = sigmoid_gate * (1.0 + gate_pre * (1.0 - sigmoid_gate))
    curvature = sigmoid_gate * (1.0 - sigmoid_gate) * (2.0 + gate_pre * (1.0 - 2.0 * sigmoid_gate))
    return (activation, slope_gate, curvature)


def swap_core(value):
    return lax.ppermute(value, "mp", [(i, i ^ 1) for i in range(4)])


def swap_chip(value):
    return lax.ppermute(value, "mp", [(i, i ^ 2) for i in range(4)])


def load_call(weights, after, name):
    n = len(weights)
    parts = 4

    def body(*refs):
        sources, targets, sems = refs[:n], refs[n + 1 : 2 * n + 1], refs[-1]
        copies = []
        for i in range(n):
            rows = sources[i].shape[0] // parts
            for j in range(parts):
                span = pl.ds(j * rows, rows)
                copies.append(
                    pltpu.make_async_copy(
                        sources[i].at[span], targets[i].at[span], sems.at[i, j]
                    )
                )
        for copy in copies:
            copy.start()
        for copy in copies:
            copy.wait()

    size = sum(w.size * 2 for w in weights)
    return pl.pallas_call(
        body,
        in_specs=[IN_HBM] * n + [pl.BlockSpec(memory_space=pl.ANY)],
        out_specs=[IN_VMEM] * n,
        out_shape=[pltpu.VMEM(w.shape, w.dtype) for w in weights],
        scratch_shapes=[pltpu.SemaphoreType.DMA((n, parts))],
        compiler_params=params(1),
        cost_estimate=cost(0, 2 * size),
        name=name,
    )(*[kept_out(w) for w in weights], after)


def norm_call(tokens, norm_gain, copies, col_width):
    own, features = tokens.shape

    def body(tokens_ref, gain_ref, out_ref, tokens_in, gain_in, scaled, sems):
        loads = [
            pltpu.make_async_copy(tokens_ref, tokens_in, sems.at[0]),
            pltpu.make_async_copy(gain_ref, gain_in, sems.at[1]),
        ]
        for load in loads:
            load.start()
        for load in loads:
            load.wait()
        tokens_f = tokens_in[...].astype(f32)
        squares = jnp.sum(tokens_f * tokens_f, axis=1, keepdims=True)
        scaled[...] = tokens_f * lax.rsqrt(squares / features + epsilon) * gain_in[...]
        first = pl.multiple_of(lax.axis_index("mp") * col_width, col_width)
        mine = scaled[:, pl.ds(first, col_width)].astype(bf16)
        for i in range(copies):
            out_ref[i] = mine

    return pl.pallas_call(
        body,
        in_specs=[IN_HBM] * 2,
        out_specs=IN_VMEM,
        out_shape=jax.ShapeDtypeStruct((copies, own, col_width), bf16),
        scratch_shapes=[
            pltpu.VMEM((own, features), bf16),
            pltpu.VMEM((1, features), f32),
            pltpu.VMEM((own, features), f32),
            pltpu.SemaphoreType.DMA((2,)),
        ],
        compiler_params=params(4),
        cost_estimate=cost(WAIT_FLOPS, 4 * own * features),
        name="norm_rows",
    )(kept_out(tokens), kept_out(norm_gain.reshape(1, features)))


def join_call(blocks):
    n = len(blocks)
    lead = sum(b[0].shape[0] for b in blocks)
    own = blocks[0][0].shape[1]
    cols = [b.shape[2] for b in blocks[0]]
    whole = len(cols) == 1

    def body(*refs):
        a_ref, b_ref = refs[-2:]
        at = 0
        for block, k in zip(blocks, range(0, n * len(cols), len(cols))):
            size = block[0].shape[0]
            if whole:
                half = cols[0] // 2
                a_ref[at : at + size] = refs[k][:, :, :half]
                b_ref[at : at + size] = refs[k][:, :, half:]
            else:
                a_ref[at : at + size] = refs[k][...]
                b_ref[at : at + size] = refs[k + 1][...]
            at += size

    half = cols[0] // 2 if whole else cols[0]
    shape = jax.ShapeDtypeStruct((lead, own, half), bf16)
    flat = [part for block in blocks for part in block]
    return pl.pallas_call(
        body,
        in_specs=[IN_VMEM] * len(flat),
        out_specs=[IN_VMEM] * 2,
        out_shape=[shape, shape],
        compiler_params=params(4),
        cost_estimate=cost(WAIT_FLOPS, 8 * lead * own * half),
        name="join",
    )(*flat)


def order_call(a_blocks, b_blocks):
    _, own, half = a_blocks[0].shape

    def body(a0, a1, b0, b1, out_ref):
        index = lax.axis_index("dp")
        for refs, order, cols in (
            ((a0, a1), (0, 4, 2, 6, 1, 5, 3, 7), slice(0, half)),
            ((b0, b1), (0, 4, 1, 5, 2, 6, 3, 7), slice(half, 2 * half)),
        ):
            for p, flip in enumerate(order):
                out_ref[lax.bitwise_xor(index, flip), :, cols] = refs[p // 4][p % 4]

    return pl.pallas_call(
        body,
        in_specs=[IN_VMEM] * 4,
        out_specs=IN_VMEM,
        out_shape=jax.ShapeDtypeStruct((8, own, 2 * half), bf16),
        compiler_params=params(4),
        cost_estimate=cost(0, 64 * own * half),
        name="token_order",
    )(*a_blocks, *b_blocks)


def gather_tree(block):
    arrived = swap_dp(block, 4)
    a_two, b_two = join_call([[block], [arrived]])
    a_came, b_came = swap_dp(a_two, 2), swap_dp(b_two, 1)
    a_four, b_four = join_call([[a_two, b_two], [a_came, b_came]])
    a_came, b_came = swap_dp(a_four, 1), swap_dp(b_four, 2)
    return order_call((a_four, a_came), (b_four, b_came))


def gate_call(normed, w_gate, w_up, v_gate, chunk, chunks):
    count, depth = normed.shape
    half = count // 2
    width = w_gate.shape[1] // chunks
    block = block_of(width, 256)
    first = chunk * (width // block)

    def body(normed_ref, gate_ref, up_ref, tan_ref, keep_ref, send_ref):
        upper = lax.axis_index("mp") % 2 == 1
        for i, weight in enumerate((gate_ref, up_ref, tan_ref)):
            part = dot(normed_ref[...], weight[...], 1, 0)
            low, high = part[:half], part[half:]
            keep_ref[i] = jnp.where(upper, high, low)
            send_ref[i] = jnp.where(upper, low, high).astype(bf16)

    weight_spec = pl.BlockSpec((depth, block), lambda i: (0, first + i))
    part_spec = pl.BlockSpec((3, half, block), lambda i: (0, 0, i))
    return pl.pallas_call(
        body,
        grid=(width // block,),
        in_specs=[pl.BlockSpec((count, depth), lambda i: (0, 0)), weight_spec, weight_spec, weight_spec],
        out_specs=[part_spec, part_spec],
        out_shape=[
            jax.ShapeDtypeStruct((3, half, width), f32),
            jax.ShapeDtypeStruct((3, half, width), bf16),
        ],
        compiler_params=params(20),
        cost_estimate=cost(6 * count * depth * width, 6 * depth * width),
        name="gate_products",
    )(normed, *[kept_out(w) for w in (w_gate, w_up, v_gate)])


def gate_held_call(normed, w_gate, w_up, v_gate, chunk, chunks, after):
    count, depth = normed.shape
    half = count // 2
    width = w_gate.shape[1] // chunks
    block = block_of(width, 512)
    steps = width // block
    first = chunk * width

    def body(normed_ref, gate_ref, up_ref, tan_ref, after_ref, keep_ref, send_ref, buffer, sems):
        copies = [
            pltpu.make_async_copy(
                tan_ref.at[:, pl.ds(first + j * block, block)], buffer.at[j], sems.at[j]
            )
            for j in range(steps)
        ]
        for copy in copies:
            copy.start()
        upper = lax.axis_index("mp") % 2 == 1
        for i, weight in enumerate((gate_ref, up_ref, None)):
            for j in range(steps):
                span = slice(j * block, (j + 1) * block)
                if weight is None:
                    copies[j].wait()
                    right = buffer[j]
                else:
                    right = weight[:, first + j * block : first + (j + 1) * block]
                part = dot(normed_ref[...], right, 1, 0)
                low, high = part[:half], part[half:]
                keep_ref[i, :, span] = jnp.where(upper, high, low)
                send_ref[i, :, span] = jnp.where(upper, low, high).astype(bf16)

    return pl.pallas_call(
        body,
        in_specs=[IN_VMEM] * 3 + [IN_HBM, pl.BlockSpec(memory_space=pl.ANY)],
        out_specs=[IN_VMEM] * 2,
        out_shape=[
            jax.ShapeDtypeStruct((3, half, width), f32),
            jax.ShapeDtypeStruct((3, half, width), bf16),
        ],
        scratch_shapes=[
            pltpu.VMEM((steps, depth, block), bf16),
            pltpu.SemaphoreType.DMA((steps,)),
        ],
        compiler_params=params(4 + 2 * depth * width // MIB),
        cost_estimate=cost(6 * count * depth * width, 6 * depth * width),
        name="gate_products",
    )(normed, held(w_gate), held(w_up), kept_out(v_gate), after)


def hidden_call(chip_sum, arrived, after):
    shape = chip_sum.shape[1:]
    width = shape[1]
    block = block_of(width, 512)

    def body(sum_ref, arrived_ref, after_ref, mine_ref, factor_ref):
        for j in range(width // block):
            span = slice(j * block, (j + 1) * block)
            gate_pre, up_value, tangent = [
                sum_ref[i, :, span] + arrived_ref[i, :, span].astype(f32) for i in range(3)
            ]
            activation, slope_gate, curvature = silu_parts(gate_pre)
            mine_ref[0, :, span] = (activation * up_value).astype(bf16)
            mine_ref[1, :, span] = (slope_gate * up_value * tangent).astype(bf16)
            factor_ref[0, :, span] = up_value * slope_gate
            factor_ref[1, :, span] = up_value * curvature * tangent

    return pl.pallas_call(
        body,
        in_specs=[IN_VMEM, IN_VMEM, pl.BlockSpec(memory_space=pl.ANY)],
        out_specs=[IN_VMEM] * 2,
        out_shape=[
            jax.ShapeDtypeStruct((2,) + shape, bf16),
            jax.ShapeDtypeStruct((2,) + shape, f32),
        ],
        compiler_params=params(8),
        cost_estimate=cost(0, 30 * shape[0] * width),
        name="hidden_units",
    )(chip_sum, arrived, after)


def down_call(mine, other, w_down, v_down):
    half, rows = mine.shape[1:]
    count = 2 * half
    features = w_down.shape[1]
    block = block_of(features, 512)

    def body(mine_ref, other_ref, w_ref, v_ref, out_ref, left):
        for i in range(2):
            left[i * count : i * count + half] = mine_ref[i]
            left[i * count + half : (i + 1) * count] = other_ref[i]
        for j in range(features // block):
            span = slice(j * block, (j + 1) * block)
            both = dot(left[...], w_ref[:, span], 1, 0)
            out_ref[0, :, span] = both[:count].astype(bf16)
            out_ref[1, :, span] = (both[count:] + dot(left[:count], v_ref[:, span], 1, 0)).astype(bf16)

    return pl.pallas_call(
        body,
        in_specs=[IN_VMEM] * 4,
        out_specs=IN_VMEM,
        out_shape=jax.ShapeDtypeStruct((2, count, features), bf16),
        scratch_shapes=[pltpu.VMEM((2 * count, rows), bf16)],
        compiler_params=params(12),
        cost_estimate=cost(6 * count * rows * features, 4 * rows * features),
        name="down_products",
    )(mine, other, held(w_down), held(v_down))


def back_call(residuals, w_down, v_down):
    count, features = residuals.shape[1:]
    half = count // 2
    rows = w_down.shape[0]
    block = block_of(rows, 512)

    def body(res_ref, w_ref, v_ref, keep_ref, send_ref, right):
        right[...] = res_ref[...].reshape(2 * count, features).T
        for j in range(rows // block):
            span = slice(j * block, (j + 1) * block)
            both = dot(w_ref[span, :], right[...], 1, 0)
            tangent = both[:, count:] + dot(v_ref[span, :], right[:, :count], 1, 0)
            for i, part in enumerate((both[:, :count].T, tangent.T)):
                keep_ref[i, :, span] = part[:half]
                send_ref[i, :, span] = part[half:].astype(bf16)

    return pl.pallas_call(
        body,
        in_specs=[IN_VMEM] * 3,
        out_specs=[IN_VMEM] * 2,
        out_shape=[
            jax.ShapeDtypeStruct((2, half, rows), f32),
            jax.ShapeDtypeStruct((2, half, rows), bf16),
        ],
        scratch_shapes=[pltpu.VMEM((features, 2 * count), bf16)],
        compiler_params=params(12),
        cost_estimate=cost(6 * count * rows * features, 4 * rows * features),
        name="back_products",
    )(residuals, held(w_down), held(v_down))


def down_score_call(mine, other, residuals, v_down):
    half, rows = mine.shape[1:]
    count = 2 * half
    features = v_down.shape[1]
    block = block_of(rows, 512)
    steps = rows // block

    def body(mine_ref, other_ref, res_ref, v_ref, out_ref, buffer, sems):
        copies = []
        for j in range(steps):
            span = slice(j * block, (j + 1) * block)
            if j >= 2:
                copies[j - 2].wait()
            left = jnp.concatenate(
                [mine_ref[1, :, span], other_ref[1, :, span], mine_ref[0, :, span], other_ref[0, :, span]],
                axis=0,
            )
            hess = dot(left, res_ref[...].reshape(2 * count, features), 0, 0)
            buffer[j % 2] = (v_ref[span, :].astype(f32) * hess).astype(bf16)
            copies.append(
                pltpu.make_async_copy(
                    buffer.at[j % 2], out_ref.at[pl.ds(j * block, block)], sems.at[j % 2]
                )
            )
            copies[j].start()
        for copy in copies[-2:]:
            copy.wait()

    return pl.pallas_call(
        body,
        in_specs=[IN_VMEM] * 4,
        out_specs=IN_HBM,
        out_shape=jax.ShapeDtypeStruct((rows, features), bf16),
        scratch_shapes=[
            pltpu.VMEM((2, block, features), bf16),
            pltpu.SemaphoreType.DMA((2,)),
        ],
        compiler_params=params(16),
        cost_estimate=cost(4 * count * rows * features, 4 * rows * features),
        name="down_score",
    )(mine, other, residuals, held(v_down))


def combine_call(chip_sum, arrived, factors, after):
    half, width = chip_sum.shape[1:]
    block = block_of(width, 512)

    def body(sum_ref, arrived_ref, factor_ref, after_ref, out_ref):
        for j in range(width // block):
            span = slice(j * block, (j + 1) * block)
            back_grad, back_tangent = [
                sum_ref[i, :, span] + arrived_ref[i, :, span].astype(f32) for i in range(2)
            ]
            out_ref[:, span] = (
                back_tangent * factor_ref[0, :, span] + back_grad * factor_ref[1, :, span]
            ).astype(bf16)

    return pl.pallas_call(
        body,
        in_specs=[IN_VMEM] * 3 + [pl.BlockSpec(memory_space=pl.ANY)],
        out_specs=IN_VMEM,
        out_shape=jax.ShapeDtypeStruct((half, width), bf16),
        compiler_params=params(8),
        cost_estimate=cost(0, 22 * half * width),
        name="combined",
    )(chip_sum, arrived, factors, kept_out(after))


def gate_score_call(normed, mine, other, v_gate):
    count, depth = normed.shape
    half = count // 2
    width = v_gate.shape[1]
    block = block_of(width, 512)
    steps = width // block

    def body(normed_ref, mine_ref, other_ref, v_ref, out_ref, buffer, sems):
        upper = lax.axis_index("mp") % 2 == 1
        copies = []
        for j in range(steps):
            span = slice(j * block, (j + 1) * block)
            if j >= 2:
                copies[j - 2].wait()
            low = jnp.where(upper, other_ref[:, span], mine_ref[:, span])
            high = jnp.where(upper, mine_ref[:, span], other_ref[:, span])
            hess = dot(normed_ref[...], jnp.concatenate([low, high], axis=0), 0, 0)
            buffer[j % 2] = (v_ref[:, span].astype(f32) * hess).astype(bf16)
            copies.append(
                pltpu.make_async_copy(
                    buffer.at[j % 2], out_ref.at[:, pl.ds(j * block, block)], sems.at[j % 2]
                )
            )
            copies[j].start()
        for copy in copies[-2:]:
            copy.wait()

    return pl.pallas_call(
        body,
        in_specs=[IN_VMEM] * 4,
        out_specs=IN_HBM,
        out_shape=jax.ShapeDtypeStruct((depth, width), bf16),
        scratch_shapes=[
            pltpu.VMEM((2, depth, block), bf16),
            pltpu.SemaphoreType.DMA((2,)),
        ],
        compiler_params=params(16),
        cost_estimate=cost(2 * count * depth * width, 4 * depth * width),
        name="gate_score",
    )(normed, mine, other, v_gate)


def bits():
    index = lax.axis_index("dp")
    return index % 2, (index // 2) % 2


def swap_dp(value, bit):
    return lax.ppermute(value, "dp", [(i, i ^ bit) for i in range(8)])


def piece_call(mine, other, w_down, v_down, away, dtype):
    half, rows = mine.shape[1:]
    count = 2 * half
    features = w_down.shape[1]
    piece = features // 8

    def body(mine_ref, other_ref, w_ref, v_ref, a_ref, b_ref, left):
        y, z = bits()
        for i in range(2):
            left[i * count : i * count + half] = mine_ref[i]
            left[i * count + half : (i + 1) * count] = other_ref[i]
        for out_ref, base, outer, inner in ((a_ref, 0, y, z), (b_ref, 4, z, y)):
            group = 1 - outer if away else outer
            for k, low in enumerate((1 - inner, inner)):
                first = pl.multiple_of((base + 2 * group + low) * piece, piece)
                both = dot(left[...], w_ref[:, pl.ds(first, piece)], 1, 0)
                tangent = both[count:] + dot(left[:count], v_ref[:, pl.ds(first, piece)], 1, 0)
                out_ref[k, 0] = both[:count].astype(dtype)
                out_ref[k, 1] = tangent.astype(dtype)

    shape = jax.ShapeDtypeStruct((2, 2, count, piece), dtype)
    return pl.pallas_call(
        body,
        in_specs=[IN_VMEM] * 4,
        out_specs=[IN_VMEM] * 2,
        out_shape=[shape, shape],
        scratch_shapes=[pltpu.VMEM((2 * count, rows), bf16)],
        compiler_params=params(8),
        cost_estimate=cost(3 * count * rows * features, 2 * rows * features),
        name="pieces_away" if away else "pieces_home",
    )(mine, other, held(w_down), held(v_down))


def residual_call(sums, arrived, target):
    count, features = target.shape
    half = count // 2
    piece = features // 8

    def body(sums_ref, arrived_ref, target_ref, a_ref, b_ref):
        y, z = bits()
        upper = lax.axis_index("mp") % 2 == 1
        for i, (out_ref, outer, inner) in enumerate(((a_ref, y, z), (b_ref, z, y))):
            first = pl.multiple_of((4 * i + 2 * outer + inner) * piece, piece)
            wanted = target_ref[:, pl.ds(first, piece)].astype(f32)
            low, high = wanted[:half], wanted[half:]
            wanted = jnp.concatenate(
                [jnp.where(upper, high, low), jnp.where(upper, low, high)], axis=0
            )
            out_ref[0] = ((sums_ref[i, 0] + arrived_ref[i, 0].astype(f32) - wanted) / count).astype(bf16)
            out_ref[1] = ((sums_ref[i, 1] + arrived_ref[i, 1].astype(f32)) / count).astype(bf16)

    shape = jax.ShapeDtypeStruct((2, count, piece), bf16)
    return pl.pallas_call(
        body,
        in_specs=[IN_VMEM] * 3,
        out_specs=[IN_VMEM] * 2,
        out_shape=[shape, shape],
        compiler_params=params(4),
        cost_estimate=cost(0, 8 * 2 * count * piece),
        name="residuals",
    )(sums, arrived, target)


def back_first_call(a_pieces, b_pieces, w_down, v_down):
    count, piece = a_pieces.shape[2:]
    rows = w_down.shape[0]
    block = block_of(rows, 512)

    def body(a_ref, b_ref, w_ref, v_ref, out_ref, right):
        y, z = bits()
        for i, (ref, inner) in enumerate(((a_ref, z), (b_ref, y))):
            for k, low in enumerate((inner, 1 - inner)):
                first = pl.multiple_of((2 * i + low) * piece, piece)
                right[pl.ds(first, piece), :] = ref[k].reshape(2 * count, piece).T
        starts = [
            pl.multiple_of(2 * piece * y, 2 * piece),
            pl.multiple_of(2 * piece * (2 + z), 2 * piece),
        ]
        for j in range(rows // block):
            span = slice(j * block, (j + 1) * block)
            total = jnp.zeros((block, 2 * count), f32)
            tangent = jnp.zeros((block, count), f32)
            for i, first in enumerate(starts):
                part = right[2 * i * piece : 2 * (i + 1) * piece]
                total += dot(w_ref[span, pl.ds(first, 2 * piece)], part, 1, 0)
                tangent += dot(v_ref[span, pl.ds(first, 2 * piece)], part[:, :count], 1, 0)
            out_ref[span] = jnp.concatenate([total[:, :count], total[:, count:] + tangent], axis=1)

    return pl.pallas_call(
        body,
        in_specs=[IN_VMEM] * 4,
        out_specs=IN_VMEM,
        out_shape=jax.ShapeDtypeStruct((rows, 2 * count), f32),
        scratch_shapes=[pltpu.VMEM((4 * piece, 2 * count), bf16)],
        compiler_params=params(8),
        cost_estimate=cost(12 * count * rows * piece, 8 * rows * piece),
        name="back_first",
    )(a_pieces, b_pieces, held(w_down), held(v_down))


def back_second_call(a_pieces, b_pieces, a_far, b_far, first_part, w_down, v_down):
    count, piece = a_pieces.shape[2:]
    half = count // 2
    rows, features = w_down.shape
    block = block_of(rows, 512)

    def body(a_ref, b_ref, a_far_ref, b_far_ref, part_ref, w_ref, v_ref, keep_ref, send_ref, res_ref, right):
        y, z = bits()
        for i, (ref, far_ref, outer, inner) in enumerate(((a_ref, a_far_ref, y, z), (b_ref, b_far_ref, z, y))):
            for k, low in enumerate((inner, 1 - inner)):
                first = pl.multiple_of((2 * i + low) * piece, piece)
                right[pl.ds(first, piece), :] = far_ref[k].reshape(2 * count, piece).T
                near = pl.multiple_of((4 * i + 2 * outer + low) * piece, piece)
                far = pl.multiple_of((4 * i + 2 * (1 - outer) + low) * piece, piece)
                for t in range(2):
                    res_ref[t, :, pl.ds(near, piece)] = ref[k, t]
                    res_ref[t, :, pl.ds(far, piece)] = far_ref[k, t]
        starts = [
            pl.multiple_of(2 * piece * (1 - y), 2 * piece),
            pl.multiple_of(2 * piece * (3 - z), 2 * piece),
        ]
        for j in range(rows // block):
            span = slice(j * block, (j + 1) * block)
            total = part_ref[span]
            tangent = jnp.zeros((block, count), f32)
            for i, first in enumerate(starts):
                part = right[2 * i * piece : 2 * (i + 1) * piece]
                total += dot(w_ref[span, pl.ds(first, 2 * piece)], part, 1, 0)
                tangent += dot(v_ref[span, pl.ds(first, 2 * piece)], part[:, :count], 1, 0)
            for i, value in enumerate((total[:, :count].T, (total[:, count:] + tangent).T)):
                keep_ref[i, :, span] = value[:half]
                send_ref[i, :, span] = value[half:].astype(bf16)

    return pl.pallas_call(
        body,
        in_specs=[IN_VMEM] * 7,
        out_specs=[IN_VMEM] * 3,
        out_shape=[
            jax.ShapeDtypeStruct((2, half, rows), f32),
            jax.ShapeDtypeStruct((2, half, rows), bf16),
            jax.ShapeDtypeStruct((2, count, features), bf16),
        ],
        scratch_shapes=[pltpu.VMEM((4 * piece, 2 * count), bf16)],
        compiler_params=params(8),
        cost_estimate=cost(12 * count * rows * piece, 8 * rows * piece),
        name="back_second",
    )(a_pieces, b_pieces, a_far, b_far, first_part, held(w_down), held(v_down))


def middle_tree(mine, other, target, w_down, v_down):
    a_send, b_send = piece_call(mine, other, w_down, v_down, True, bf16)
    a_recv, b_recv = swap_dp(a_send, 1), swap_dp(b_send, 2)
    a_home, b_home = piece_call(mine, other, w_down, v_down, False, f32)
    a_sum = a_home + a_recv.astype(f32)
    b_sum = b_home + b_recv.astype(f32)
    a_recv, b_recv = swap_dp(a_sum[0].astype(bf16), 2), swap_dp(b_sum[0].astype(bf16), 1)
    sums = jnp.stack([a_sum[1] + a_recv.astype(f32), b_sum[1] + b_recv.astype(f32)])
    arrived = swap_dp(sums.astype(bf16), 4)
    a_res, b_res = residual_call(sums, arrived, target)
    a_pieces = jnp.stack([a_res, swap_dp(a_res, 2)])
    b_pieces = jnp.stack([b_res, swap_dp(b_res, 1)])
    a_far, b_far = swap_dp(a_pieces, 1), swap_dp(b_pieces, 2)
    first_part = back_first_call(a_pieces, b_pieces, w_down, v_down)
    return back_second_call(a_pieces, b_pieces, a_far, b_far, first_part, w_down, v_down)


def middle_direct(dp, mine, other, target, w_down, v_down):
    half = mine.shape[1]
    count = 2 * half
    own = count // dp
    features = w_down.shape[1]
    out_parts = down_call(mine, other, w_down, v_down)
    pieces = out_parts.reshape(2, dp, own, features).swapaxes(0, 1)
    arrived = lax.all_to_all(pieces, "dp", 0, 0, tiled=True).astype(f32)
    totals = jnp.sum(arrived, axis=0)
    core = lax.axis_index("mp") % 2
    first_row = (lax.axis_index("dp") * own + core * half) % count
    target_rows = lax.dynamic_slice_in_dim(target, first_row, own, 0)
    residual_rows = ((totals[0] - target_rows.astype(f32)) / count).astype(bf16)
    residual_tan_rows = (totals[1] / count).astype(bf16)
    rows = jnp.stack([residual_rows, residual_tan_rows])
    spread = lax.all_to_all(
        jnp.broadcast_to(rows[None], (dp,) + rows.shape), "dp", 0, 0, tiled=True
    )
    residuals = spread.swapaxes(0, 1).reshape(2, count, features)
    keep, send = back_call(residuals, w_down, v_down)
    return keep, send, residuals


def per_device(dp, tokens, norm_gain, target, w_gate, w_up, v_gate, w_down, v_down):
    own = tokens.shape[0]
    count = own * dp
    col_width = w_gate.shape[0]
    if dp == 8:
        block = norm_call(tokens, norm_gain, 1, col_width)
        normed = gather_tree(block).reshape(count, col_width)
        keep, send = gate_held_call(normed, w_gate, w_up, v_gate, 0, 1, normed)
    else:
        copies = norm_call(tokens, norm_gain, dp, col_width)
        normed = lax.all_to_all(copies, "dp", 0, 0, tiled=True).reshape(count, col_width)
        keep, send = gate_call(normed, w_gate, w_up, v_gate, 0, 1)
    chip_sum = keep + swap_core(send).astype(f32)
    chip_send = chip_sum.astype(bf16)
    w_down, v_down = load_call([w_down, v_down], chip_send, "load_down")
    mine, factors = hidden_call(chip_sum, swap_chip(chip_send), held(v_down))
    other = swap_core(mine)
    if dp == 8:
        keep, send, residuals = middle_tree(mine, other, target, w_down, v_down)
    else:
        keep, send, residuals = middle_direct(dp, mine, other, target, w_down, v_down)
    chip_sum = keep + swap_core(send).astype(f32)
    arrived = swap_chip(chip_sum.astype(bf16))
    down_score = down_score_call(mine, other, residuals, v_down)
    combined = combine_call(chip_sum, arrived, factors, down_score)
    gate_score = gate_score_call(normed, combined, swap_core(combined), v_gate)
    return (gate_score, down_score)


def solution(mesh):
    in_specs = (
        P("dp", None),
        P(),
        P(None, "mp"),
        P("mp", "dp"),
        P("mp", "dp"),
        P("mp", "dp"),
        P("dp", "mp"),
        P("dp", "mp"),
    )
    out_specs = (P("mp", "dp"), P("dp", "mp"))
    return jax.shard_map(
        functools.partial(per_device, mesh.shape["dp"]),
        mesh=mesh,
        in_specs=in_specs,
        out_specs=out_specs,
        check_vma=False,
    )
```

```python
import functools
import math
import jax
import jax.numpy as jnp
from jax import lax
from jax.experimental import pallas as pl
from jax.experimental.pallas import tpu as pltpu
from jax.sharding import PartitionSpec as P

epsilon = 1e-06
bf16 = jnp.bfloat16
f32 = jnp.float32
MIB = 1024 * 1024
WAIT_FLOPS = 6 * 10**9
CHUNKS = 3
BACK_CHUNKS = 2
BUFFERS = 4
IN_VMEM = pl.BlockSpec(memory_space=pltpu.VMEM)
IN_HBM = pl.BlockSpec(memory_space=pltpu.HBM)


def block_of(extent, most):
    size = most
    while extent % size:
        size -= 128
    return size


def params(mebibytes):
    return pltpu.CompilerParams(vmem_limit_bytes=mebibytes * MIB)


def cost(flops, bytes_accessed):
    return pl.CostEstimate(flops=flops, bytes_accessed=bytes_accessed, transcendentals=0)


def dot(left, right, left_dim, right_dim):
    return lax.dot_general(
        left, right, (((left_dim,), (right_dim,)), ((), ())), preferred_element_type=f32
    )


def order(operands, in_specs, after):
    if after is not None:
        operands.append(after)
        in_specs.append(pl.BlockSpec(memory_space=pl.ANY))


def held(value):
    return pltpu.with_memory_space_constraint(value, pltpu.VMEM)


def kept_out(value):
    return pltpu.with_memory_space_constraint(value, pltpu.HBM)


def join_hidden(refs, left):
    at = 0
    for mine_ref, other_ref in zip(refs[::2], refs[1::2]):
        _, half, width = mine_ref.shape
        for i in range(2):
            left[2 * i * half : (2 * i + 1) * half, at : at + width] = mine_ref[i]
            left[(2 * i + 1) * half : (2 * i + 2) * half, at : at + width] = other_ref[i]
        at += width


def silu_parts(gate_pre):
    sigmoid_gate = jax.nn.sigmoid(gate_pre)
    activation = gate_pre * sigmoid_gate
    slope_gate = sigmoid_gate * (1.0 + gate_pre * (1.0 - sigmoid_gate))
    curvature = sigmoid_gate * (1.0 - sigmoid_gate) * (2.0 + gate_pre * (1.0 - 2.0 * sigmoid_gate))
    return (activation, slope_gate, curvature)


def swap_core(value):
    return lax.ppermute(value, "mp", [(i, i ^ 1) for i in range(4)])


def swap_chip(value):
    return lax.ppermute(value, "mp", [(i, i ^ 2) for i in range(4)])


def load_call(weights, after, name):
    n = len(weights)
    parts = 4

    def body(*refs):
        sources, targets, sems = refs[:n], refs[n + 1 : 2 * n + 1], refs[-1]
        copies = []
        for i in range(n):
            rows = sources[i].shape[0] // parts
            for j in range(parts):
                span = pl.ds(j * rows, rows)
                copies.append(
                    pltpu.make_async_copy(
                        sources[i].at[span], targets[i].at[span], sems.at[i, j]
                    )
                )
        for copy in copies:
            copy.start()
        for copy in copies:
            copy.wait()

    size = sum(w.size * 2 for w in weights)
    return pl.pallas_call(
        body,
        in_specs=[IN_HBM] * n + [pl.BlockSpec(memory_space=pl.ANY)],
        out_specs=[IN_VMEM] * n,
        out_shape=[pltpu.VMEM(w.shape, w.dtype) for w in weights],
        scratch_shapes=[pltpu.SemaphoreType.DMA((n, parts))],
        compiler_params=params(1),
        cost_estimate=cost(0, 2 * size),
        name=name,
    )(*[kept_out(w) for w in weights], after)


def norm_call(tokens, norm_gain, copies, col_width):
    own, features = tokens.shape

    def body(tokens_ref, gain_ref, out_ref, tokens_in, gain_in, scaled, sems):
        loads = [
            pltpu.make_async_copy(tokens_ref, tokens_in, sems.at[0]),
            pltpu.make_async_copy(gain_ref, gain_in, sems.at[1]),
        ]
        for load in loads:
            load.start()
        for load in loads:
            load.wait()
        tokens_f = tokens_in[...].astype(f32)
        squares = jnp.sum(tokens_f * tokens_f, axis=1, keepdims=True)
        scaled[...] = tokens_f * lax.rsqrt(squares / features + epsilon) * gain_in[...]
        first = pl.multiple_of(lax.axis_index("mp") * col_width, col_width)
        mine = scaled[:, pl.ds(first, col_width)].astype(bf16)
        for i in range(copies):
            out_ref[i] = mine

    return pl.pallas_call(
        body,
        in_specs=[IN_HBM] * 2,
        out_specs=IN_VMEM,
        out_shape=jax.ShapeDtypeStruct((copies, own, col_width), bf16),
        scratch_shapes=[
            pltpu.VMEM((own, features), bf16),
            pltpu.VMEM((1, features), f32),
            pltpu.VMEM((own, features), f32),
            pltpu.SemaphoreType.DMA((2,)),
        ],
        compiler_params=params(4),
        cost_estimate=cost(WAIT_FLOPS, 4 * own * features),
        name="norm_rows",
    )(kept_out(tokens), kept_out(norm_gain.reshape(1, features)))


def join_call(blocks):
    n = len(blocks)
    lead = sum(b[0].shape[0] for b in blocks)
    own = blocks[0][0].shape[1]
    cols = [b.shape[2] for b in blocks[0]]
    whole = len(cols) == 1

    def body(*refs):
        a_ref, b_ref = refs[-2:]
        at = 0
        for block, k in zip(blocks, range(0, n * len(cols), len(cols))):
            size = block[0].shape[0]
            if whole:
                half = cols[0] // 2
                a_ref[at : at + size] = refs[k][:, :, :half]
                b_ref[at : at + size] = refs[k][:, :, half:]
            else:
                a_ref[at : at + size] = refs[k][...]
                b_ref[at : at + size] = refs[k + 1][...]
            at += size

    half = cols[0] // 2 if whole else cols[0]
    shape = jax.ShapeDtypeStruct((lead, own, half), bf16)
    flat = [part for block in blocks for part in block]
    return pl.pallas_call(
        body,
        in_specs=[IN_VMEM] * len(flat),
        out_specs=[IN_VMEM] * 2,
        out_shape=[shape, shape],
        compiler_params=params(4),
        cost_estimate=cost(WAIT_FLOPS, 8 * lead * own * half),
        name="join",
    )(*flat)


def order_call(a_blocks, b_blocks):
    _, own, half = a_blocks[0].shape

    def body(a0, a1, b0, b1, out_ref):
        index = lax.axis_index("dp")
        for refs, order, cols in (
            ((a0, a1), (0, 4, 2, 6, 1, 5, 3, 7), slice(0, half)),
            ((b0, b1), (0, 4, 1, 5, 2, 6, 3, 7), slice(half, 2 * half)),
        ):
            for p, flip in enumerate(order):
                out_ref[lax.bitwise_xor(index, flip), :, cols] = refs[p // 4][p % 4]

    return pl.pallas_call(
        body,
        in_specs=[IN_VMEM] * 4,
        out_specs=IN_VMEM,
        out_shape=jax.ShapeDtypeStruct((8, own, 2 * half), bf16),
        compiler_params=params(4),
        cost_estimate=cost(0, 64 * own * half),
        name="token_order",
    )(*a_blocks, *b_blocks)


def gather_tree(block):
    arrived = swap_dp(block, 4)
    a_two, b_two = join_call([[block], [arrived]])
    a_came, b_came = swap_dp(a_two, 2), swap_dp(b_two, 1)
    a_four, b_four = join_call([[a_two, b_two], [a_came, b_came]])
    a_came, b_came = swap_dp(a_four, 1), swap_dp(b_four, 2)
    return order_call((a_four, a_came), (b_four, b_came))


def gate_call(normed, w_gate, w_up, v_gate, chunk, chunks):
    count, depth = normed.shape
    half = count // 2
    width = w_gate.shape[1] // chunks
    block = block_of(width, 256)
    first = chunk * (width // block)

    def body(normed_ref, gate_ref, up_ref, tan_ref, keep_ref, send_ref):
        upper = lax.axis_index("mp") % 2 == 1
        for i, weight in enumerate((gate_ref, up_ref, tan_ref)):
            part = dot(normed_ref[...], weight[...], 1, 0)
            low, high = part[:half], part[half:]
            keep_ref[i] = jnp.where(upper, high, low)
            send_ref[i] = jnp.where(upper, low, high).astype(bf16)

    weight_spec = pl.BlockSpec((depth, block), lambda i: (0, first + i))
    part_spec = pl.BlockSpec((3, half, block), lambda i: (0, 0, i))
    return pl.pallas_call(
        body,
        grid=(width // block,),
        in_specs=[pl.BlockSpec((count, depth), lambda i: (0, 0)), weight_spec, weight_spec, weight_spec],
        out_specs=[part_spec, part_spec],
        out_shape=[
            jax.ShapeDtypeStruct((3, half, width), f32),
            jax.ShapeDtypeStruct((3, half, width), bf16),
        ],
        compiler_params=params(20),
        cost_estimate=cost(6 * count * depth * width, 6 * depth * width),
        name="gate_products",
    )(normed, *[kept_out(w) for w in (w_gate, w_up, v_gate)])


def gate_held_call(normed, w_gate, w_up, v_gate, chunk, chunks, after):
    count, depth = normed.shape
    half = count // 2
    width = w_gate.shape[1] // chunks
    block = block_of(width, 512)
    steps = width // block
    first = chunk * width

    def body(normed_ref, gate_ref, up_ref, tan_ref, *rest):
        keep_ref, send_ref, buffer, sems = rest[-4:]
        copies = [
            pltpu.make_async_copy(
                tan_ref.at[:, pl.ds(first + j * block, block)], buffer.at[j], sems.at[j]
            )
            for j in range(steps)
        ]
        for copy in copies:
            copy.start()
        upper = lax.axis_index("mp") % 2 == 1
        for i, weight in enumerate((gate_ref, up_ref, None)):
            for j in range(steps):
                span = slice(j * block, (j + 1) * block)
                if weight is None:
                    copies[j].wait()
                    right = buffer[j]
                else:
                    right = weight[:, first + j * block : first + (j + 1) * block]
                part = dot(normed_ref[...], right, 1, 0)
                low, high = part[:half], part[half:]
                keep_ref[i, :, span] = jnp.where(upper, high, low)
                send_ref[i, :, span] = jnp.where(upper, low, high).astype(bf16)

    operands = [normed, held(w_gate), held(w_up), kept_out(v_gate)]
    in_specs = [IN_VMEM] * 3 + [IN_HBM]
    order(operands, in_specs, after)
    return pl.pallas_call(
        body,
        in_specs=in_specs,
        out_specs=[IN_VMEM] * 2,
        out_shape=[
            jax.ShapeDtypeStruct((3, half, width), f32),
            jax.ShapeDtypeStruct((3, half, width), bf16),
        ],
        scratch_shapes=[
            pltpu.VMEM((steps, depth, block), bf16),
            pltpu.SemaphoreType.DMA((steps,)),
        ],
        compiler_params=params(4 + 2 * depth * width // MIB),
        cost_estimate=cost(6 * count * depth * width, 6 * depth * width),
        name="gate_products",
    )(*operands)


def hidden_call(chip_sum, arrived, after):
    shape = chip_sum.shape[1:]
    width = shape[1]
    block = block_of(width, 512)

    def body(sum_ref, arrived_ref, *rest):
        mine_ref, factor_ref = rest[-2:]
        for j in range(width // block):
            span = slice(j * block, (j + 1) * block)
            gate_pre, up_value, tangent = [
                sum_ref[i, :, span] + arrived_ref[i, :, span].astype(f32) for i in range(3)
            ]
            activation, slope_gate, curvature = silu_parts(gate_pre)
            mine_ref[0, :, span] = (activation * up_value).astype(bf16)
            mine_ref[1, :, span] = (slope_gate * up_value * tangent).astype(bf16)
            factor_ref[0, :, span] = up_value * slope_gate
            factor_ref[1, :, span] = up_value * curvature * tangent

    operands, in_specs = [chip_sum, arrived], [IN_VMEM] * 2
    order(operands, in_specs, after)
    return pl.pallas_call(
        body,
        in_specs=in_specs,
        out_specs=[IN_VMEM] * 2,
        out_shape=[
            jax.ShapeDtypeStruct((2,) + shape, bf16),
            jax.ShapeDtypeStruct((2,) + shape, f32),
        ],
        compiler_params=params(8),
        cost_estimate=cost(0, 30 * shape[0] * width),
        name="hidden_units",
    )(*operands)


def down_call(hiddens, w_down, v_down):
    count = 2 * hiddens[0].shape[1]
    rows, features = w_down.shape
    block = block_of(features, 512)
    n = len(hiddens)

    def body(*refs):
        w_ref, v_ref, out_ref, left = refs[n:]
        join_hidden(refs[:n], left)
        for j in range(features // block):
            span = slice(j * block, (j + 1) * block)
            both = dot(left[...], w_ref[:, span], 1, 0)
            out_ref[0, :, span] = both[:count].astype(bf16)
            out_ref[1, :, span] = (both[count:] + dot(left[:count], v_ref[:, span], 1, 0)).astype(bf16)

    return pl.pallas_call(
        body,
        in_specs=[IN_VMEM] * (n + 2),
        out_specs=IN_VMEM,
        out_shape=jax.ShapeDtypeStruct((2, count, features), bf16),
        scratch_shapes=[pltpu.VMEM((2 * count, rows), bf16)],
        compiler_params=params(12),
        cost_estimate=cost(6 * count * rows * features, 4 * rows * features),
        name="down_products",
    )(*hiddens, held(w_down), held(v_down))


def back_call(residuals, w_down, v_down):
    count, features = residuals.shape[1:]
    half = count // 2
    rows = w_down.shape[0]
    block = block_of(rows, 512)

    def body(res_ref, w_ref, v_ref, keep_ref, send_ref, right):
        right[...] = res_ref[...].reshape(2 * count, features).T
        for j in range(rows // block):
            span = slice(j * block, (j + 1) * block)
            both = dot(w_ref[span, :], right[...], 1, 0)
            tangent = both[:, count:] + dot(v_ref[span, :], right[:, :count], 1, 0)
            for i, part in enumerate((both[:, :count].T, tangent.T)):
                keep_ref[i, :, span] = part[:half]
                send_ref[i, :, span] = part[half:].astype(bf16)

    return pl.pallas_call(
        body,
        in_specs=[IN_VMEM] * 3,
        out_specs=[IN_VMEM] * 2,
        out_shape=[
            jax.ShapeDtypeStruct((2, half, rows), f32),
            jax.ShapeDtypeStruct((2, half, rows), bf16),
        ],
        scratch_shapes=[pltpu.VMEM((features, 2 * count), bf16)],
        compiler_params=params(12),
        cost_estimate=cost(6 * count * rows * features, 4 * rows * features),
        name="back_products",
    )(residuals, held(w_down), held(v_down))


def down_score_call(hiddens, residuals, v_down):
    rows, features = v_down.shape
    count = residuals.shape[1]
    block = block_of(rows, 512)
    steps = rows // block
    n = len(hiddens)

    def body(*refs):
        res_ref, v_ref, out_ref, left, right, buffer, sems = refs[n:]
        join_hidden(refs[:n], left)
        right[:count] = res_ref[1]
        right[count:] = res_ref[0]
        copies = []
        for j in range(steps):
            span = slice(j * block, (j + 1) * block)
            if j >= BUFFERS:
                copies[j - BUFFERS].wait()
            hess = dot(left[:, span], right[...], 0, 0)
            buffer[j % BUFFERS] = (v_ref[span, :].astype(f32) * hess).astype(bf16)
            copies.append(
                pltpu.make_async_copy(
                    buffer.at[j % BUFFERS], out_ref.at[pl.ds(j * block, block)], sems.at[j % BUFFERS]
                )
            )
            copies[j].start()
        for copy in copies[-BUFFERS:]:
            copy.wait()

    return pl.pallas_call(
        body,
        in_specs=[IN_VMEM] * (n + 2),
        out_specs=IN_HBM,
        out_shape=jax.ShapeDtypeStruct((rows, features), bf16),
        scratch_shapes=[
            pltpu.VMEM((2 * count, rows), bf16),
            pltpu.VMEM((2 * count, features), bf16),
            pltpu.VMEM((BUFFERS, block, features), bf16),
            pltpu.SemaphoreType.DMA((BUFFERS,)),
        ],
        compiler_params=params(20),
        cost_estimate=cost(4 * count * rows * features, 4 * rows * features),
        name="down_score",
    )(*hiddens, residuals, held(v_down))


def combine_call(chip_sum, arrived, factors, chunk, after):
    half, width = chip_sum.shape[1:]
    part = factors[0].shape[2]
    block = block_of(math.gcd(width, part), 512)
    n = len(factors)

    def body(sum_ref, arrived_ref, *rest):
        factor_refs, out_ref = rest[:n], rest[-1]
        for j in range(width // block):
            span = slice(j * block, (j + 1) * block)
            back_grad, back_tangent = [
                sum_ref[i, :, span] + arrived_ref[i, :, span].astype(f32) for i in range(2)
            ]
            at = chunk * width + j * block
            factor_ref, start = factor_refs[at // part], at % part
            taken = slice(start, start + block)
            out_ref[:, span] = (
                back_tangent * factor_ref[0, :, taken] + back_grad * factor_ref[1, :, taken]
            ).astype(bf16)

    return pl.pallas_call(
        body,
        in_specs=[IN_VMEM] * (n + 2) + [pl.BlockSpec(memory_space=pl.ANY)],
        out_specs=IN_VMEM,
        out_shape=jax.ShapeDtypeStruct((half, width), bf16),
        compiler_params=params(8),
        cost_estimate=cost(0, 22 * half * width),
        name="combined",
    )(chip_sum, arrived, *factors, kept_out(after))


def gate_score_call(normed, combined, v_gate):
    count, depth = normed.shape
    half = count // 2
    width = v_gate.shape[1]
    part = combined[0].shape[1]
    block = block_of(part, 512)
    steps = width // block
    n = len(combined)

    def body(normed_ref, *rest):
        v_ref, out_ref, buffer, sems = rest[n:]
        upper = lax.axis_index("mp") % 2 == 1
        copies = []
        for j in range(steps):
            span = slice(j * block, (j + 1) * block)
            at = j * block // part
            taken = slice(j * block % part, j * block % part + block)
            mine, other = rest[2 * at][:, taken], rest[2 * at + 1][:, taken]
            if j >= BUFFERS:
                copies[j - BUFFERS].wait()
            low = jnp.where(upper, other, mine)
            high = jnp.where(upper, mine, other)
            hess = dot(normed_ref[...], jnp.concatenate([low, high], axis=0), 0, 0)
            buffer[j % BUFFERS] = (v_ref[:, span].astype(f32) * hess).astype(bf16)
            copies.append(
                pltpu.make_async_copy(
                    buffer.at[j % BUFFERS], out_ref.at[:, pl.ds(j * block, block)], sems.at[j % BUFFERS]
                )
            )
            copies[j].start()
        for copy in copies[-BUFFERS:]:
            copy.wait()

    return pl.pallas_call(
        body,
        in_specs=[IN_VMEM] * (n + 2),
        out_specs=IN_HBM,
        out_shape=jax.ShapeDtypeStruct((depth, width), bf16),
        scratch_shapes=[
            pltpu.VMEM((BUFFERS, depth, block), bf16),
            pltpu.SemaphoreType.DMA((BUFFERS,)),
        ],
        compiler_params=params(20),
        cost_estimate=cost(2 * count * depth * width, 4 * depth * width),
        name="gate_score",
    )(normed, *combined, held(v_gate))


def bits():
    index = lax.axis_index("dp")
    return index % 2, (index // 2) % 2


def swap_dp(value, bit):
    return lax.ppermute(value, "dp", [(i, i ^ bit) for i in range(8)])


def piece_call(hiddens, w_down, v_down, away, dtype):
    count = 2 * hiddens[0].shape[1]
    rows, features = w_down.shape
    n = len(hiddens)
    piece = features // 8

    def body(*refs):
        w_ref, v_ref, a_ref, b_ref, left = refs[n:]
        y, z = bits()
        join_hidden(refs[:n], left)
        for out_ref, base, outer, inner in ((a_ref, 0, y, z), (b_ref, 4, z, y)):
            group = 1 - outer if away else outer
            for k, low in enumerate((1 - inner, inner)):
                first = pl.multiple_of((base + 2 * group + low) * piece, piece)
                both = dot(left[...], w_ref[:, pl.ds(first, piece)], 1, 0)
                tangent = both[count:] + dot(left[:count], v_ref[:, pl.ds(first, piece)], 1, 0)
                out_ref[k, 0] = both[:count].astype(dtype)
                out_ref[k, 1] = tangent.astype(dtype)

    shape = jax.ShapeDtypeStruct((2, 2, count, piece), dtype)
    return pl.pallas_call(
        body,
        in_specs=[IN_VMEM] * (n + 2),
        out_specs=[IN_VMEM] * 2,
        out_shape=[shape, shape],
        scratch_shapes=[pltpu.VMEM((2 * count, rows), bf16)],
        compiler_params=params(8),
        cost_estimate=cost(3 * count * rows * features, 2 * rows * features),
        name="pieces_away" if away else "pieces_home",
    )(*hiddens, held(w_down), held(v_down))


def residual_call(sums, arrived, target):
    count, features = target.shape
    half = count // 2
    piece = features // 8

    def body(sums_ref, arrived_ref, target_ref, a_ref, b_ref):
        y, z = bits()
        upper = lax.axis_index("mp") % 2 == 1
        for i, (out_ref, outer, inner) in enumerate(((a_ref, y, z), (b_ref, z, y))):
            first = pl.multiple_of((4 * i + 2 * outer + inner) * piece, piece)
            wanted = target_ref[:, pl.ds(first, piece)].astype(f32)
            low, high = wanted[:half], wanted[half:]
            wanted = jnp.concatenate(
                [jnp.where(upper, high, low), jnp.where(upper, low, high)], axis=0
            )
            out_ref[0] = ((sums_ref[i, 0] + arrived_ref[i, 0].astype(f32) - wanted) / count).astype(bf16)
            out_ref[1] = ((sums_ref[i, 1] + arrived_ref[i, 1].astype(f32)) / count).astype(bf16)

    shape = jax.ShapeDtypeStruct((2, count, piece), bf16)
    return pl.pallas_call(
        body,
        in_specs=[IN_VMEM] * 3,
        out_specs=[IN_VMEM] * 2,
        out_shape=[shape, shape],
        compiler_params=params(4),
        cost_estimate=cost(0, 8 * 2 * count * piece),
        name="residuals",
    )(sums, arrived, target)


def back_first_call(a_pieces, b_pieces, w_down, v_down):
    count, piece = a_pieces.shape[2:]
    rows = w_down.shape[0]
    block = block_of(rows, 512)

    def body(a_ref, b_ref, w_ref, v_ref, out_ref, right):
        y, z = bits()
        for i, (ref, inner) in enumerate(((a_ref, z), (b_ref, y))):
            for k, low in enumerate((inner, 1 - inner)):
                first = pl.multiple_of((2 * i + low) * piece, piece)
                right[pl.ds(first, piece), :] = ref[k].reshape(2 * count, piece).T
        starts = [
            pl.multiple_of(2 * piece * y, 2 * piece),
            pl.multiple_of(2 * piece * (2 + z), 2 * piece),
        ]
        for j in range(rows // block):
            span = slice(j * block, (j + 1) * block)
            total = jnp.zeros((block, 2 * count), f32)
            tangent = jnp.zeros((block, count), f32)
            for i, first in enumerate(starts):
                part = right[2 * i * piece : 2 * (i + 1) * piece]
                total += dot(w_ref[span, pl.ds(first, 2 * piece)], part, 1, 0)
                tangent += dot(v_ref[span, pl.ds(first, 2 * piece)], part[:, :count], 1, 0)
            out_ref[span] = jnp.concatenate([total[:, :count], total[:, count:] + tangent], axis=1)

    return pl.pallas_call(
        body,
        in_specs=[IN_VMEM] * 4,
        out_specs=IN_VMEM,
        out_shape=jax.ShapeDtypeStruct((rows, 2 * count), f32),
        scratch_shapes=[pltpu.VMEM((4 * piece, 2 * count), bf16)],
        compiler_params=params(8),
        cost_estimate=cost(12 * count * rows * piece, 8 * rows * piece),
        name="back_first",
    )(a_pieces, b_pieces, held(w_down), held(v_down))


def back_second_call(a_pieces, b_pieces, a_far, b_far, first_part, w_down, v_down, chunk, chunks):
    count, piece = a_pieces.shape[2:]
    half = count // 2
    features = w_down.shape[1]
    rows = w_down.shape[0] // chunks
    block = block_of(rows, 512)
    from_row = chunk * rows

    def body(a_ref, b_ref, a_far_ref, b_far_ref, part_ref, w_ref, v_ref, keep_ref, send_ref, *rest):
        right = rest[-1]
        y, z = bits()
        for i, (ref, far_ref, outer, inner) in enumerate(((a_ref, a_far_ref, y, z), (b_ref, b_far_ref, z, y))):
            for k, low in enumerate((inner, 1 - inner)):
                first = pl.multiple_of((2 * i + low) * piece, piece)
                right[pl.ds(first, piece), :] = far_ref[k].reshape(2 * count, piece).T
                if chunk == 0:
                    near = pl.multiple_of((4 * i + 2 * outer + low) * piece, piece)
                    far = pl.multiple_of((4 * i + 2 * (1 - outer) + low) * piece, piece)
                    for t in range(2):
                        rest[0][t, :, pl.ds(near, piece)] = ref[k, t]
                        rest[0][t, :, pl.ds(far, piece)] = far_ref[k, t]
        starts = [
            pl.multiple_of(2 * piece * (1 - y), 2 * piece),
            pl.multiple_of(2 * piece * (3 - z), 2 * piece),
        ]
        for j in range(rows // block):
            span = slice(j * block, (j + 1) * block)
            taken = slice(from_row + j * block, from_row + (j + 1) * block)
            total = part_ref[taken]
            tangent = jnp.zeros((block, count), f32)
            for i, first in enumerate(starts):
                part = right[2 * i * piece : 2 * (i + 1) * piece]
                total += dot(w_ref[taken, pl.ds(first, 2 * piece)], part, 1, 0)
                tangent += dot(v_ref[taken, pl.ds(first, 2 * piece)], part[:, :count], 1, 0)
            for i, value in enumerate((total[:, :count].T, (total[:, count:] + tangent).T)):
                keep_ref[i, :, span] = value[:half]
                send_ref[i, :, span] = value[half:].astype(bf16)

    out_shape = [
        jax.ShapeDtypeStruct((2, half, rows), f32),
        jax.ShapeDtypeStruct((2, half, rows), bf16),
    ]
    if chunk == 0:
        out_shape.append(jax.ShapeDtypeStruct((2, count, features), bf16))
    return pl.pallas_call(
        body,
        in_specs=[IN_VMEM] * 7,
        out_specs=[IN_VMEM] * len(out_shape),
        out_shape=out_shape,
        scratch_shapes=[pltpu.VMEM((4 * piece, 2 * count), bf16)],
        compiler_params=params(8),
        cost_estimate=cost(12 * count * rows * piece, 8 * rows * piece),
        name="back_second",
    )(a_pieces, b_pieces, a_far, b_far, first_part, held(w_down), held(v_down))


def middle_tree(hiddens, target, w_down, v_down, chunks):
    a_send, b_send = piece_call(hiddens, w_down, v_down, True, bf16)
    a_recv, b_recv = swap_dp(a_send, 1), swap_dp(b_send, 2)
    a_home, b_home = piece_call(hiddens, w_down, v_down, False, f32)
    a_sum = a_home + a_recv.astype(f32)
    b_sum = b_home + b_recv.astype(f32)
    a_recv, b_recv = swap_dp(a_sum[0].astype(bf16), 2), swap_dp(b_sum[0].astype(bf16), 1)
    sums = jnp.stack([a_sum[1] + a_recv.astype(f32), b_sum[1] + b_recv.astype(f32)])
    arrived = swap_dp(sums.astype(bf16), 4)
    a_res, b_res = residual_call(sums, arrived, target)
    a_pieces = jnp.stack([a_res, swap_dp(a_res, 2)])
    b_pieces = jnp.stack([b_res, swap_dp(b_res, 1)])
    a_far, b_far = swap_dp(a_pieces, 1), swap_dp(b_pieces, 2)
    first_part = back_first_call(a_pieces, b_pieces, w_down, v_down)
    parts = [
        back_second_call(a_pieces, b_pieces, a_far, b_far, first_part, w_down, v_down, chunk, chunks)
        for chunk in range(chunks)
    ]
    return [chip_sum_of(part[:2]) for part in parts], parts[0][2]


def middle_direct(dp, hiddens, target, w_down, v_down):
    half = hiddens[0].shape[1]
    count = 2 * half
    own = count // dp
    features = w_down.shape[1]
    out_parts = down_call(hiddens, w_down, v_down)
    pieces = out_parts.reshape(2, dp, own, features).swapaxes(0, 1)
    arrived = lax.all_to_all(pieces, "dp", 0, 0, tiled=True).astype(f32)
    totals = jnp.sum(arrived, axis=0)
    core = lax.axis_index("mp") % 2
    first_row = (lax.axis_index("dp") * own + core * half) % count
    target_rows = lax.dynamic_slice_in_dim(target, first_row, own, 0)
    residual_rows = ((totals[0] - target_rows.astype(f32)) / count).astype(bf16)
    residual_tan_rows = (totals[1] / count).astype(bf16)
    rows = jnp.stack([residual_rows, residual_tan_rows])
    spread = lax.all_to_all(
        jnp.broadcast_to(rows[None], (dp,) + rows.shape), "dp", 0, 0, tiled=True
    )
    residuals = spread.swapaxes(0, 1).reshape(2, count, features)
    return [chip_sum_of(back_call(residuals, w_down, v_down))], residuals


def chip_sum_of(product):
    keep, send = product
    chip_sum = keep + swap_core(send).astype(f32)
    return chip_sum, chip_sum.astype(bf16)


def per_device(dp, tokens, norm_gain, target, w_gate, w_up, v_gate, w_down, v_down):
    own = tokens.shape[0]
    count = own * dp
    col_width = w_gate.shape[0]
    chunks, back_chunks = (CHUNKS, BACK_CHUNKS) if dp == 8 else (1, 1)
    if dp == 8:
        block = norm_call(tokens, norm_gain, 1, col_width)
        normed = gather_tree(block).reshape(count, col_width)
        sums = []
        for chunk in range(chunks):
            after = sums[chunk - 2][1] if chunk > 1 else None
            products = gate_held_call(normed, w_gate, w_up, v_gate, chunk, chunks, after)
            sums.append(chip_sum_of(products))
    else:
        copies = norm_call(tokens, norm_gain, dp, col_width)
        normed = lax.all_to_all(copies, "dp", 0, 0, tiled=True).reshape(count, col_width)
        sums = [chip_sum_of(gate_call(normed, w_gate, w_up, v_gate, 0, 1))]
    arrived = [swap_chip(send) for _, send in sums]
    waits = [None] * chunks
    if dp == 8:
        w_down, v_down = load_call([w_down, v_down], sums[-1][1], "load_down")
        waits = [w_down] * chunks
    hiddens, factors = [], []
    for chunk, ((chip_sum, _), came, wait) in enumerate(zip(sums, arrived, waits)):
        mine, factor = hidden_call(chip_sum, came, None if wait is None else held(wait))
        hiddens += [mine, swap_core(mine)]
        factors.append(factor)
    if dp == 8:
        sums, residuals = middle_tree(hiddens, target, w_down, v_down, back_chunks)
    else:
        sums, residuals = middle_direct(dp, hiddens, target, w_down, v_down)
    arrived = [swap_chip(send) for _, send in sums]
    down_score = down_score_call(hiddens, residuals, v_down)
    combined = []
    for chunk, ((chip_sum, _), came) in enumerate(zip(sums, arrived)):
        mine = combine_call(chip_sum, came, factors, chunk, down_score)
        combined += [mine, swap_core(mine)]
    gate_score = gate_score_call(normed, combined, v_gate)
    return (gate_score, down_score)


def solution(mesh):
    in_specs = (
        P("dp", None),
        P(),
        P(None, "mp"),
        P("mp", "dp"),
        P("mp", "dp"),
        P("mp", "dp"),
        P("dp", "mp"),
        P("dp", "mp"),
    )
    out_specs = (P("mp", "dp"), P("dp", "mp"))
    return jax.shard_map(
        functools.partial(per_device, mesh.shape["dp"]),
        mesh=mesh,
        in_specs=in_specs,
        out_specs=out_specs,
        check_vma=False,
    )
```

```python
import functools
import math
import jax
import jax.numpy as jnp
from jax import lax
from jax.experimental import pallas as pl
from jax.experimental.pallas import tpu as pltpu
from jax.sharding import PartitionSpec as P

epsilon = 1e-06
bf16 = jnp.bfloat16
f32 = jnp.float32
MIB = 1024 * 1024
WAIT_FLOPS = 15 * 10**9
CHUNKS = 3
BACK_CHUNKS = 2
BUFFERS = 4
IN_VMEM = pl.BlockSpec(memory_space=pltpu.VMEM)
IN_HBM = pl.BlockSpec(memory_space=pltpu.HBM)


def block_of(extent, most):
    size = most
    while extent % size:
        size -= 128
    return size


def params(mebibytes):
    return pltpu.CompilerParams(vmem_limit_bytes=mebibytes * MIB)


def cost(flops, bytes_accessed):
    return pl.CostEstimate(flops=flops, bytes_accessed=bytes_accessed, transcendentals=0)


def dot(left, right, left_dim, right_dim):
    return lax.dot_general(
        left, right, (((left_dim,), (right_dim,)), ((), ())), preferred_element_type=f32
    )


def order(operands, in_specs, after):
    if after is not None:
        operands.append(after)
        in_specs.append(pl.BlockSpec(memory_space=pl.ANY))


def held(value):
    return pltpu.with_memory_space_constraint(value, pltpu.VMEM)


def kept_out(value):
    return pltpu.with_memory_space_constraint(value, pltpu.HBM)


def join_hidden(refs, left):
    at = 0
    for mine_ref, other_ref in zip(refs[::2], refs[1::2]):
        _, half, width = mine_ref.shape
        for i in range(2):
            left[2 * i * half : (2 * i + 1) * half, at : at + width] = mine_ref[i]
            left[(2 * i + 1) * half : (2 * i + 2) * half, at : at + width] = other_ref[i]
        at += width


def silu_parts(gate_pre):
    sigmoid_gate = jax.nn.sigmoid(gate_pre)
    activation = gate_pre * sigmoid_gate
    slope_gate = sigmoid_gate * (1.0 + gate_pre * (1.0 - sigmoid_gate))
    curvature = sigmoid_gate * (1.0 - sigmoid_gate) * (2.0 + gate_pre * (1.0 - 2.0 * sigmoid_gate))
    return (activation, slope_gate, curvature)


def swap_core(value):
    return lax.ppermute(value, "mp", [(i, i ^ 1) for i in range(4)])


def swap_chip(value):
    return lax.ppermute(value, "mp", [(i, i ^ 2) for i in range(4)])


def load_call(weights, after, name, shares=1):
    n = len(weights)
    shapes = [(w.shape[0], w.shape[1] // shares) for w in weights]
    parts = 4

    def body(*refs):
        sources, targets, sems = refs[:n], refs[n + 1 : 2 * n + 1], refs[-1]
        copies = []
        for i in range(n):
            rows = sources[i].shape[0] // parts
            for j in range(parts):
                span = pl.ds(j * rows, rows)
                copies.append(
                    pltpu.make_async_copy(
                        sources[i].at[span, pl.ds(0, shapes[i][1])], targets[i].at[span], sems.at[i, j]
                    )
                )
        for copy in copies:
            copy.start()
        for copy in copies:
            copy.wait()

    size = sum(w.size * 2 for w in weights) // shares
    return pl.pallas_call(
        body,
        in_specs=[IN_HBM] * n + [pl.BlockSpec(memory_space=pl.ANY)],
        out_specs=[IN_VMEM] * n,
        out_shape=[pltpu.VMEM(shape, w.dtype) for shape, w in zip(shapes, weights)],
        scratch_shapes=[pltpu.SemaphoreType.DMA((n, parts))],
        compiler_params=params(1),
        cost_estimate=cost(0, 2 * size),
        name=name,
    )(*[kept_out(w) for w in weights], after)


def norm_call(tokens, norm_gain, copies, col_width):
    own, features = tokens.shape

    def body(tokens_ref, gain_ref, out_ref, tokens_in, gain_in, scaled, sems):
        loads = [
            pltpu.make_async_copy(tokens_ref, tokens_in, sems.at[0]),
            pltpu.make_async_copy(gain_ref, gain_in, sems.at[1]),
        ]
        for load in loads:
            load.start()
        for load in loads:
            load.wait()
        tokens_f = tokens_in[...].astype(f32)
        squares = jnp.sum(tokens_f * tokens_f, axis=1, keepdims=True)
        scaled[...] = tokens_f * lax.rsqrt(squares / features + epsilon) * gain_in[...]
        first = pl.multiple_of(lax.axis_index("mp") * col_width, col_width)
        mine = scaled[:, pl.ds(first, col_width)].astype(bf16)
        for i in range(copies):
            out_ref[i] = mine

    return pl.pallas_call(
        body,
        in_specs=[IN_HBM] * 2,
        out_specs=IN_VMEM,
        out_shape=jax.ShapeDtypeStruct((copies, own, col_width), bf16),
        scratch_shapes=[
            pltpu.VMEM((own, features), bf16),
            pltpu.VMEM((1, features), f32),
            pltpu.VMEM((own, features), f32),
            pltpu.SemaphoreType.DMA((2,)),
        ],
        compiler_params=params(4),
        cost_estimate=cost(WAIT_FLOPS, 4 * own * features),
        name="norm_rows",
    )(kept_out(tokens), kept_out(norm_gain.reshape(1, features)))


def join_call(blocks):
    n = len(blocks)
    lead = sum(b[0].shape[0] for b in blocks)
    own = blocks[0][0].shape[1]
    cols = [b.shape[2] for b in blocks[0]]
    whole = len(cols) == 1

    def body(*refs):
        a_ref, b_ref = refs[-2:]
        at = 0
        for block, k in zip(blocks, range(0, n * len(cols), len(cols))):
            size = block[0].shape[0]
            if whole:
                half = cols[0] // 2
                a_ref[at : at + size] = refs[k][:, :, :half]
                b_ref[at : at + size] = refs[k][:, :, half:]
            else:
                a_ref[at : at + size] = refs[k][...]
                b_ref[at : at + size] = refs[k + 1][...]
            at += size

    half = cols[0] // 2 if whole else cols[0]
    shape = jax.ShapeDtypeStruct((lead, own, half), bf16)
    flat = [part for block in blocks for part in block]
    return pl.pallas_call(
        body,
        in_specs=[IN_VMEM] * len(flat),
        out_specs=[IN_VMEM] * 2,
        out_shape=[shape, shape],
        compiler_params=params(4),
        cost_estimate=cost(WAIT_FLOPS, 8 * lead * own * half),
        name="join",
    )(*flat)


def order_call(a_blocks, b_blocks, after):
    _, own, half = a_blocks[0].shape

    def body(a0, a1, b0, b1, after_ref, out_ref):
        index = lax.axis_index("dp")
        for refs, order, cols in (
            ((a0, a1), (0, 4, 2, 6, 1, 5, 3, 7), slice(0, half)),
            ((b0, b1), (0, 4, 1, 5, 2, 6, 3, 7), slice(half, 2 * half)),
        ):
            for p, flip in enumerate(order):
                out_ref[lax.bitwise_xor(index, flip), :, cols] = refs[p // 4][p % 4]

    return pl.pallas_call(
        body,
        in_specs=[IN_VMEM] * 4 + [pl.BlockSpec(memory_space=pl.ANY)],
        out_specs=IN_VMEM,
        out_shape=jax.ShapeDtypeStruct((8, own, 2 * half), bf16),
        compiler_params=params(4),
        cost_estimate=cost(0, 64 * own * half),
        name="token_order",
    )(*a_blocks, *b_blocks, after)


def gather_tree(block, v_gate, chunks):
    arrived = swap_dp(block, 4)
    a_two, b_two = join_call([[block], [arrived]])
    a_came, b_came = swap_dp(a_two, 2), swap_dp(b_two, 1)
    a_four, b_four = join_call([[a_two, b_two], [a_came, b_came]])
    a_came, b_came = swap_dp(a_four, 1), swap_dp(b_four, 2)
    (first,) = load_call([v_gate], a_four, "load_first", chunks)
    return order_call((a_four, a_came), (b_four, b_came), held(first)), first


def gate_call(normed, w_gate, w_up, v_gate, chunk, chunks):
    count, depth = normed.shape
    half = count // 2
    width = w_gate.shape[1] // chunks
    block = block_of(width, 256)
    first = chunk * (width // block)

    def body(normed_ref, gate_ref, up_ref, tan_ref, keep_ref, send_ref):
        upper = lax.axis_index("mp") % 2 == 1
        for i, weight in enumerate((gate_ref, up_ref, tan_ref)):
            part = dot(normed_ref[...], weight[...], 1, 0)
            low, high = part[:half], part[half:]
            keep_ref[i] = jnp.where(upper, high, low)
            send_ref[i] = jnp.where(upper, low, high).astype(bf16)

    weight_spec = pl.BlockSpec((depth, block), lambda i: (0, first + i))
    part_spec = pl.BlockSpec((3, half, block), lambda i: (0, 0, i))
    return pl.pallas_call(
        body,
        grid=(width // block,),
        in_specs=[pl.BlockSpec((count, depth), lambda i: (0, 0)), weight_spec, weight_spec, weight_spec],
        out_specs=[part_spec, part_spec],
        out_shape=[
            jax.ShapeDtypeStruct((3, half, width), f32),
            jax.ShapeDtypeStruct((3, half, width), bf16),
        ],
        compiler_params=params(20),
        cost_estimate=cost(6 * count * depth * width, 6 * depth * width),
        name="gate_products",
    )(normed, *[kept_out(w) for w in (w_gate, w_up, v_gate)])


def gate_held_call(normed, w_gate, w_up, v_gate, first_probe, chunk, chunks, after):
    count, depth = normed.shape
    half = count // 2
    width = w_gate.shape[1] // chunks
    block = block_of(width, 512)
    steps = width // block
    first = chunk * width

    def body(normed_ref, gate_ref, up_ref, tan_ref, *rest):
        keep_ref, send_ref, buffer, sems = rest[-4:]
        copies = [
            pltpu.make_async_copy(
                tan_ref.at[:, pl.ds(first + j * block, block)], buffer.at[j], sems.at[j]
            )
            for j in range(0 if chunk == 0 else steps)
        ]
        for copy in copies:
            copy.start()
        upper = lax.axis_index("mp") % 2 == 1
        for i, weight in enumerate((gate_ref, up_ref, None)):
            for j in range(steps):
                span = slice(j * block, (j + 1) * block)
                if weight is None and chunk == 0:
                    right = tan_ref[:, span]
                elif weight is None:
                    copies[j].wait()
                    right = buffer[j]
                else:
                    right = weight[:, first + j * block : first + (j + 1) * block]
                part = dot(normed_ref[...], right, 1, 0)
                low, high = part[:half], part[half:]
                keep_ref[i, :, span] = jnp.where(upper, high, low)
                send_ref[i, :, span] = jnp.where(upper, low, high).astype(bf16)

    probe = held(first_probe) if chunk == 0 else kept_out(v_gate)
    operands = [normed, held(w_gate), held(w_up), probe]
    in_specs = [IN_VMEM] * 3 + [IN_VMEM if chunk == 0 else IN_HBM]
    order(operands, in_specs, after)
    return pl.pallas_call(
        body,
        in_specs=in_specs,
        out_specs=[IN_VMEM] * 2,
        out_shape=[
            jax.ShapeDtypeStruct((3, half, width), f32),
            jax.ShapeDtypeStruct((3, half, width), bf16),
        ],
        scratch_shapes=[
            pltpu.VMEM((steps, depth, block), bf16),
            pltpu.SemaphoreType.DMA((steps,)),
        ],
        compiler_params=params(4 + 2 * depth * width // MIB),
        cost_estimate=cost(6 * count * depth * width, 6 * depth * width),
        name="gate_products",
    )(*operands)


def hidden_call(chip_sum, arrived, after):
    shape = chip_sum.shape[1:]
    width = shape[1]
    block = block_of(width, 512)

    def body(sum_ref, arrived_ref, *rest):
        mine_ref, factor_ref = rest[-2:]
        for j in range(width // block):
            span = slice(j * block, (j + 1) * block)
            gate_pre, up_value, tangent = [
                sum_ref[i, :, span] + arrived_ref[i, :, span].astype(f32) for i in range(3)
            ]
            activation, slope_gate, curvature = silu_parts(gate_pre)
            mine_ref[0, :, span] = (activation * up_value).astype(bf16)
            mine_ref[1, :, span] = (slope_gate * up_value * tangent).astype(bf16)
            factor_ref[0, :, span] = up_value * slope_gate
            factor_ref[1, :, span] = up_value * curvature * tangent

    operands, in_specs = [chip_sum, arrived], [IN_VMEM] * 2
    order(operands, in_specs, after)
    return pl.pallas_call(
        body,
        in_specs=in_specs,
        out_specs=[IN_VMEM] * 2,
        out_shape=[
            jax.ShapeDtypeStruct((2,) + shape, bf16),
            jax.ShapeDtypeStruct((2,) + shape, f32),
        ],
        compiler_params=params(8),
        cost_estimate=cost(0, 30 * shape[0] * width),
        name="hidden_units",
    )(*operands)


def down_call(hiddens, w_down, v_down):
    count = 2 * hiddens[0].shape[1]
    rows, features = w_down.shape
    block = block_of(features, 512)
    n = len(hiddens)

    def body(*refs):
        w_ref, v_ref, out_ref, left = refs[n:]
        join_hidden(refs[:n], left)
        for j in range(features // block):
            span = slice(j * block, (j + 1) * block)
            both = dot(left[...], w_ref[:, span], 1, 0)
            out_ref[0, :, span] = both[:count].astype(bf16)
            out_ref[1, :, span] = (both[count:] + dot(left[:count], v_ref[:, span], 1, 0)).astype(bf16)

    return pl.pallas_call(
        body,
        in_specs=[IN_VMEM] * (n + 2),
        out_specs=IN_VMEM,
        out_shape=jax.ShapeDtypeStruct((2, count, features), bf16),
        scratch_shapes=[pltpu.VMEM((2 * count, rows), bf16)],
        compiler_params=params(12),
        cost_estimate=cost(6 * count * rows * features, 4 * rows * features),
        name="down_products",
    )(*hiddens, held(w_down), held(v_down))


def back_call(residuals, w_down, v_down):
    count, features = residuals.shape[1:]
    half = count // 2
    rows = w_down.shape[0]
    block = block_of(rows, 512)

    def body(res_ref, w_ref, v_ref, keep_ref, send_ref, right):
        right[...] = res_ref[...].reshape(2 * count, features).T
        for j in range(rows // block):
            span = slice(j * block, (j + 1) * block)
            both = dot(w_ref[span, :], right[...], 1, 0)
            tangent = both[:, count:] + dot(v_ref[span, :], right[:, :count], 1, 0)
            for i, part in enumerate((both[:, :count].T, tangent.T)):
                keep_ref[i, :, span] = part[:half]
                send_ref[i, :, span] = part[half:].astype(bf16)

    return pl.pallas_call(
        body,
        in_specs=[IN_VMEM] * 3,
        out_specs=[IN_VMEM] * 2,
        out_shape=[
            jax.ShapeDtypeStruct((2, half, rows), f32),
            jax.ShapeDtypeStruct((2, half, rows), bf16),
        ],
        scratch_shapes=[pltpu.VMEM((features, 2 * count), bf16)],
        compiler_params=params(12),
        cost_estimate=cost(6 * count * rows * features, 4 * rows * features),
        name="back_products",
    )(residuals, held(w_down), held(v_down))


def down_score_call(hiddens, residuals, v_down):
    rows, features = v_down.shape
    count = residuals.shape[1]
    block = block_of(rows, 512)
    steps = rows // block
    n = len(hiddens)

    def body(*refs):
        res_ref, v_ref, out_ref, left, right, buffer, sems = refs[n:]
        join_hidden(refs[:n], left)
        right[:count] = res_ref[1]
        right[count:] = res_ref[0]
        copies = []
        for j in range(steps):
            span = slice(j * block, (j + 1) * block)
            if j >= BUFFERS:
                copies[j - BUFFERS].wait()
            hess = dot(left[:, span], right[...], 0, 0)
            buffer[j % BUFFERS] = (v_ref[span, :].astype(f32) * hess).astype(bf16)
            copies.append(
                pltpu.make_async_copy(
                    buffer.at[j % BUFFERS], out_ref.at[pl.ds(j * block, block)], sems.at[j % BUFFERS]
                )
            )
            copies[j].start()
        for copy in copies[-BUFFERS:]:
            copy.wait()

    return pl.pallas_call(
        body,
        in_specs=[IN_VMEM] * (n + 2),
        out_specs=IN_HBM,
        out_shape=jax.ShapeDtypeStruct((rows, features), bf16),
        scratch_shapes=[
            pltpu.VMEM((2 * count, rows), bf16),
            pltpu.VMEM((2 * count, features), bf16),
            pltpu.VMEM((BUFFERS, block, features), bf16),
            pltpu.SemaphoreType.DMA((BUFFERS,)),
        ],
        compiler_params=params(20),
        cost_estimate=cost(4 * count * rows * features, 4 * rows * features),
        name="down_score",
    )(*hiddens, residuals, held(v_down))


def combine_call(chip_sum, arrived, factors, chunk, after):
    half, width = chip_sum.shape[1:]
    part = factors[0].shape[2]
    block = block_of(math.gcd(width, part), 512)
    n = len(factors)

    def body(sum_ref, arrived_ref, *rest):
        factor_refs, out_ref = rest[:n], rest[-1]
        for j in range(width // block):
            span = slice(j * block, (j + 1) * block)
            back_grad, back_tangent = [
                sum_ref[i, :, span] + arrived_ref[i, :, span].astype(f32) for i in range(2)
            ]
            at = chunk * width + j * block
            factor_ref, start = factor_refs[at // part], at % part
            taken = slice(start, start + block)
            out_ref[:, span] = (
                back_tangent * factor_ref[0, :, taken] + back_grad * factor_ref[1, :, taken]
            ).astype(bf16)

    return pl.pallas_call(
        body,
        in_specs=[IN_VMEM] * (n + 2) + [pl.BlockSpec(memory_space=pl.ANY)],
        out_specs=IN_VMEM,
        out_shape=jax.ShapeDtypeStruct((half, width), bf16),
        compiler_params=params(8),
        cost_estimate=cost(0, 22 * half * width),
        name="combined",
    )(chip_sum, arrived, *factors, kept_out(after))


def gate_score_call(normed, combined, v_gate):
    count, depth = normed.shape
    half = count // 2
    width = v_gate.shape[1]
    part = combined[0].shape[1]
    block = block_of(part, 512)
    steps = width // block
    n = len(combined)

    def body(normed_ref, *rest):
        v_ref, out_ref, buffer, sems = rest[n:]
        upper = lax.axis_index("mp") % 2 == 1
        copies = []
        for j in range(steps):
            span = slice(j * block, (j + 1) * block)
            at = j * block // part
            taken = slice(j * block % part, j * block % part + block)
            mine, other = rest[2 * at][:, taken], rest[2 * at + 1][:, taken]
            if j >= BUFFERS:
                copies[j - BUFFERS].wait()
            low = jnp.where(upper, other, mine)
            high = jnp.where(upper, mine, other)
            hess = dot(normed_ref[...], jnp.concatenate([low, high], axis=0), 0, 0)
            buffer[j % BUFFERS] = (v_ref[:, span].astype(f32) * hess).astype(bf16)
            copies.append(
                pltpu.make_async_copy(
                    buffer.at[j % BUFFERS], out_ref.at[:, pl.ds(j * block, block)], sems.at[j % BUFFERS]
                )
            )
            copies[j].start()
        for copy in copies[-BUFFERS:]:
            copy.wait()

    return pl.pallas_call(
        body,
        in_specs=[IN_VMEM] * (n + 2),
        out_specs=IN_HBM,
        out_shape=jax.ShapeDtypeStruct((depth, width), bf16),
        scratch_shapes=[
            pltpu.VMEM((BUFFERS, depth, block), bf16),
            pltpu.SemaphoreType.DMA((BUFFERS,)),
        ],
        compiler_params=params(20),
        cost_estimate=cost(2 * count * depth * width, 4 * depth * width),
        name="gate_score",
    )(normed, *combined, held(v_gate))


def bits():
    index = lax.axis_index("dp")
    return index % 2, (index // 2) % 2


def swap_dp(value, bit):
    return lax.ppermute(value, "dp", [(i, i ^ bit) for i in range(8)])


def piece_call(hiddens, w_down, v_down, away, dtype):
    count = 2 * hiddens[0].shape[1]
    rows, features = w_down.shape
    n = len(hiddens)
    piece = features // 8

    def body(*refs):
        w_ref, v_ref, a_ref, b_ref, left = refs[n:]
        y, z = bits()
        join_hidden(refs[:n], left)
        for out_ref, base, outer, inner in ((a_ref, 0, y, z), (b_ref, 4, z, y)):
            group = 1 - outer if away else outer
            for k, low in enumerate((1 - inner, inner)):
                first = pl.multiple_of((base + 2 * group + low) * piece, piece)
                both = dot(left[...], w_ref[:, pl.ds(first, piece)], 1, 0)
                tangent = both[count:] + dot(left[:count], v_ref[:, pl.ds(first, piece)], 1, 0)
                out_ref[k, 0] = both[:count].astype(dtype)
                out_ref[k, 1] = tangent.astype(dtype)

    shape = jax.ShapeDtypeStruct((2, 2, count, piece), dtype)
    return pl.pallas_call(
        body,
        in_specs=[IN_VMEM] * (n + 2),
        out_specs=[IN_VMEM] * 2,
        out_shape=[shape, shape],
        scratch_shapes=[pltpu.VMEM((2 * count, rows), bf16)],
        compiler_params=params(8),
        cost_estimate=cost(3 * count * rows * features, 2 * rows * features),
        name="pieces_away" if away else "pieces_home",
    )(*hiddens, held(w_down), held(v_down))


def residual_call(sums, arrived, target):
    count, features = target.shape
    half = count // 2
    piece = features // 8

    def body(sums_ref, arrived_ref, target_ref, a_ref, b_ref):
        y, z = bits()
        upper = lax.axis_index("mp") % 2 == 1
        for i, (out_ref, outer, inner) in enumerate(((a_ref, y, z), (b_ref, z, y))):
            first = pl.multiple_of((4 * i + 2 * outer + inner) * piece, piece)
            wanted = target_ref[:, pl.ds(first, piece)].astype(f32)
            low, high = wanted[:half], wanted[half:]
            wanted = jnp.concatenate(
                [jnp.where(upper, high, low), jnp.where(upper, low, high)], axis=0
            )
            out_ref[0] = ((sums_ref[i, 0] + arrived_ref[i, 0].astype(f32) - wanted) / count).astype(bf16)
            out_ref[1] = ((sums_ref[i, 1] + arrived_ref[i, 1].astype(f32)) / count).astype(bf16)

    shape = jax.ShapeDtypeStruct((2, count, piece), bf16)
    return pl.pallas_call(
        body,
        in_specs=[IN_VMEM] * 3,
        out_specs=[IN_VMEM] * 2,
        out_shape=[shape, shape],
        compiler_params=params(4),
        cost_estimate=cost(0, 8 * 2 * count * piece),
        name="residuals",
    )(sums, arrived, target)


def back_first_call(a_pieces, b_pieces, w_down, v_down):
    count, piece = a_pieces.shape[2:]
    rows = w_down.shape[0]
    block = block_of(rows, 512)

    def body(a_ref, b_ref, w_ref, v_ref, out_ref, right):
        y, z = bits()
        for i, (ref, inner) in enumerate(((a_ref, z), (b_ref, y))):
            for k, low in enumerate((inner, 1 - inner)):
                first = pl.multiple_of((2 * i + low) * piece, piece)
                right[pl.ds(first, piece), :] = ref[k].reshape(2 * count, piece).T
        starts = [
            pl.multiple_of(2 * piece * y, 2 * piece),
            pl.multiple_of(2 * piece * (2 + z), 2 * piece),
        ]
        for j in range(rows // block):
            span = slice(j * block, (j + 1) * block)
            total = jnp.zeros((block, 2 * count), f32)
            tangent = jnp.zeros((block, count), f32)
            for i, first in enumerate(starts):
                part = right[2 * i * piece : 2 * (i + 1) * piece]
                total += dot(w_ref[span, pl.ds(first, 2 * piece)], part, 1, 0)
                tangent += dot(v_ref[span, pl.ds(first, 2 * piece)], part[:, :count], 1, 0)
            out_ref[span] = jnp.concatenate([total[:, :count], total[:, count:] + tangent], axis=1)

    return pl.pallas_call(
        body,
        in_specs=[IN_VMEM] * 4,
        out_specs=IN_VMEM,
        out_shape=jax.ShapeDtypeStruct((rows, 2 * count), f32),
        scratch_shapes=[pltpu.VMEM((4 * piece, 2 * count), bf16)],
        compiler_params=params(8),
        cost_estimate=cost(12 * count * rows * piece, 8 * rows * piece),
        name="back_first",
    )(a_pieces, b_pieces, held(w_down), held(v_down))


def back_second_call(a_pieces, b_pieces, a_far, b_far, first_part, w_down, v_down, chunk, chunks):
    count, piece = a_pieces.shape[2:]
    half = count // 2
    features = w_down.shape[1]
    rows = w_down.shape[0] // chunks
    block = block_of(rows, 512)
    from_row = chunk * rows

    def body(a_ref, b_ref, a_far_ref, b_far_ref, part_ref, w_ref, v_ref, keep_ref, send_ref, *rest):
        right = rest[-1]
        y, z = bits()
        for i, (ref, far_ref, outer, inner) in enumerate(((a_ref, a_far_ref, y, z), (b_ref, b_far_ref, z, y))):
            for k, low in enumerate((inner, 1 - inner)):
                first = pl.multiple_of((2 * i + low) * piece, piece)
                right[pl.ds(first, piece), :] = far_ref[k].reshape(2 * count, piece).T
                if chunk == 0:
                    near = pl.multiple_of((4 * i + 2 * outer + low) * piece, piece)
                    far = pl.multiple_of((4 * i + 2 * (1 - outer) + low) * piece, piece)
                    for t in range(2):
                        rest[0][t, :, pl.ds(near, piece)] = ref[k, t]
                        rest[0][t, :, pl.ds(far, piece)] = far_ref[k, t]
        starts = [
            pl.multiple_of(2 * piece * (1 - y), 2 * piece),
            pl.multiple_of(2 * piece * (3 - z), 2 * piece),
        ]
        for j in range(rows // block):
            span = slice(j * block, (j + 1) * block)
            taken = slice(from_row + j * block, from_row + (j + 1) * block)
            total = part_ref[taken]
            tangent = jnp.zeros((block, count), f32)
            for i, first in enumerate(starts):
                part = right[2 * i * piece : 2 * (i + 1) * piece]
                total += dot(w_ref[taken, pl.ds(first, 2 * piece)], part, 1, 0)
                tangent += dot(v_ref[taken, pl.ds(first, 2 * piece)], part[:, :count], 1, 0)
            for i, value in enumerate((total[:, :count].T, (total[:, count:] + tangent).T)):
                keep_ref[i, :, span] = value[:half]
                send_ref[i, :, span] = value[half:].astype(bf16)

    out_shape = [
        jax.ShapeDtypeStruct((2, half, rows), f32),
        jax.ShapeDtypeStruct((2, half, rows), bf16),
    ]
    if chunk == 0:
        out_shape.append(jax.ShapeDtypeStruct((2, count, features), bf16))
    return pl.pallas_call(
        body,
        in_specs=[IN_VMEM] * 7,
        out_specs=[IN_VMEM] * len(out_shape),
        out_shape=out_shape,
        scratch_shapes=[pltpu.VMEM((4 * piece, 2 * count), bf16)],
        compiler_params=params(8),
        cost_estimate=cost(12 * count * rows * piece, 8 * rows * piece),
        name="back_second",
    )(a_pieces, b_pieces, a_far, b_far, first_part, held(w_down), held(v_down))


def middle_tree(hiddens, target, w_down, v_down, chunks):
    a_send, b_send = piece_call(hiddens, w_down, v_down, True, bf16)
    a_recv, b_recv = swap_dp(a_send, 1), swap_dp(b_send, 2)
    a_home, b_home = piece_call(hiddens, w_down, v_down, False, f32)
    a_sum = a_home + a_recv.astype(f32)
    b_sum = b_home + b_recv.astype(f32)
    a_recv, b_recv = swap_dp(a_sum[0].astype(bf16), 2), swap_dp(b_sum[0].astype(bf16), 1)
    sums = jnp.stack([a_sum[1] + a_recv.astype(f32), b_sum[1] + b_recv.astype(f32)])
    arrived = swap_dp(sums.astype(bf16), 4)
    a_res, b_res = residual_call(sums, arrived, target)
    a_pieces = jnp.stack([a_res, swap_dp(a_res, 2)])
    b_pieces = jnp.stack([b_res, swap_dp(b_res, 1)])
    a_far, b_far = swap_dp(a_pieces, 1), swap_dp(b_pieces, 2)
    first_part = back_first_call(a_pieces, b_pieces, w_down, v_down)
    parts = [
        back_second_call(a_pieces, b_pieces, a_far, b_far, first_part, w_down, v_down, chunk, chunks)
        for chunk in range(chunks)
    ]
    return [chip_sum_of(part[:2]) for part in parts], parts[0][2]


def middle_direct(dp, hiddens, target, w_down, v_down):
    half = hiddens[0].shape[1]
    count = 2 * half
    own = count // dp
    features = w_down.shape[1]
    out_parts = down_call(hiddens, w_down, v_down)
    pieces = out_parts.reshape(2, dp, own, features).swapaxes(0, 1)
    arrived = lax.all_to_all(pieces, "dp", 0, 0, tiled=True).astype(f32)
    totals = jnp.sum(arrived, axis=0)
    core = lax.axis_index("mp") % 2
    first_row = (lax.axis_index("dp") * own + core * half) % count
    target_rows = lax.dynamic_slice_in_dim(target, first_row, own, 0)
    residual_rows = ((totals[0] - target_rows.astype(f32)) / count).astype(bf16)
    residual_tan_rows = (totals[1] / count).astype(bf16)
    rows = jnp.stack([residual_rows, residual_tan_rows])
    spread = lax.all_to_all(
        jnp.broadcast_to(rows[None], (dp,) + rows.shape), "dp", 0, 0, tiled=True
    )
    residuals = spread.swapaxes(0, 1).reshape(2, count, features)
    return [chip_sum_of(back_call(residuals, w_down, v_down))], residuals


def chip_sum_of(product):
    keep, send = product
    chip_sum = keep + swap_core(send).astype(f32)
    return chip_sum, chip_sum.astype(bf16)


def per_device(dp, tokens, norm_gain, target, w_gate, w_up, v_gate, w_down, v_down):
    own = tokens.shape[0]
    count = own * dp
    col_width = w_gate.shape[0]
    chunks, back_chunks = (CHUNKS, BACK_CHUNKS) if dp == 8 else (1, 1)
    if dp == 8:
        block = norm_call(tokens, norm_gain, 1, col_width)
        normed, first = gather_tree(block, v_gate, chunks)
        normed = normed.reshape(count, col_width)
        sums = []
        for chunk in range(chunks):
            after = sums[chunk - 2][1] if chunk > 1 else None
            products = gate_held_call(
                normed, w_gate, w_up, v_gate, first, chunk, chunks, after
            )
            sums.append(chip_sum_of(products))
    else:
        copies = norm_call(tokens, norm_gain, dp, col_width)
        normed = lax.all_to_all(copies, "dp", 0, 0, tiled=True).reshape(count, col_width)
        sums = [chip_sum_of(gate_call(normed, w_gate, w_up, v_gate, 0, 1))]
    arrived = [swap_chip(send) for _, send in sums]
    waits = [None] * chunks
    if dp == 8:
        w_down, v_down = load_call([w_down, v_down], sums[-1][1], "load_down")
        waits = [None] + [w_down] * (chunks - 1)
    hiddens, factors = [], []
    for chunk, ((chip_sum, _), came, wait) in enumerate(zip(sums, arrived, waits)):
        mine, factor = hidden_call(chip_sum, came, None if wait is None else held(wait))
        hiddens += [mine, swap_core(mine)]
        factors.append(factor)
    if dp == 8:
        sums, residuals = middle_tree(hiddens, target, w_down, v_down, back_chunks)
    else:
        sums, residuals = middle_direct(dp, hiddens, target, w_down, v_down)
    arrived = [swap_chip(send) for _, send in sums]
    down_score = down_score_call(hiddens, residuals, v_down)
    combined = []
    for chunk, ((chip_sum, _), came) in enumerate(zip(sums, arrived)):
        mine = combine_call(chip_sum, came, factors, chunk, down_score)
        combined += [mine, swap_core(mine)]
    gate_score = gate_score_call(normed, combined, v_gate)
    return (gate_score, down_score)


def solution(mesh):
    in_specs = (
        P("dp", None),
        P(),
        P(None, "mp"),
        P("mp", "dp"),
        P("mp", "dp"),
        P("mp", "dp"),
        P("dp", "mp"),
        P("dp", "mp"),
    )
    out_specs = (P("mp", "dp"), P("dp", "mp"))
    return jax.shard_map(
        functools.partial(per_device, mesh.shape["dp"]),
        mesh=mesh,
        in_specs=in_specs,
        out_specs=out_specs,
        check_vma=False,
    )
```

```python
import functools
import math
import jax
import jax.numpy as jnp
from jax import lax
from jax.experimental import pallas as pl
from jax.experimental.pallas import tpu as pltpu
from jax.sharding import PartitionSpec as P

epsilon = 1e-06
bf16 = jnp.bfloat16
f32 = jnp.float32
MIB = 1024 * 1024
WAIT_FLOPS = 15 * 10**9
CHUNKS = 3
BACK_CHUNKS = 2
BUFFERS = 4
IN_VMEM = pl.BlockSpec(memory_space=pltpu.VMEM)
IN_HBM = pl.BlockSpec(memory_space=pltpu.HBM)


def block_of(extent, most):
    size = most
    while extent % size:
        size -= 128
    return size


def params(mebibytes):
    return pltpu.CompilerParams(vmem_limit_bytes=mebibytes * MIB)


def cost(flops, bytes_accessed):
    return pl.CostEstimate(flops=flops, bytes_accessed=bytes_accessed, transcendentals=0)


def dot(left, right, left_dim, right_dim):
    return lax.dot_general(
        left, right, (((left_dim,), (right_dim,)), ((), ())), preferred_element_type=f32
    )


def order(operands, in_specs, after):
    if after is not None:
        operands.append(after)
        in_specs.append(pl.BlockSpec(memory_space=pl.ANY))


def held(value):
    return pltpu.with_memory_space_constraint(value, pltpu.VMEM)


def kept_out(value):
    return pltpu.with_memory_space_constraint(value, pltpu.HBM)


def join_hidden(refs, left):
    at = 0
    for mine_ref, other_ref in zip(refs[::2], refs[1::2]):
        _, half, width = mine_ref.shape
        for i in range(2):
            left[2 * i * half : (2 * i + 1) * half, at : at + width] = mine_ref[i]
            left[(2 * i + 1) * half : (2 * i + 2) * half, at : at + width] = other_ref[i]
        at += width


def silu_parts(gate_pre):
    sigmoid_gate = jax.nn.sigmoid(gate_pre)
    activation = gate_pre * sigmoid_gate
    slope_gate = sigmoid_gate * (1.0 + gate_pre * (1.0 - sigmoid_gate))
    curvature = sigmoid_gate * (1.0 - sigmoid_gate) * (2.0 + gate_pre * (1.0 - 2.0 * sigmoid_gate))
    return (activation, slope_gate, curvature)


def swap_core(value):
    return lax.ppermute(value, "mp", [(i, i ^ 1) for i in range(4)])


def swap_chip(value):
    return lax.ppermute(value, "mp", [(i, i ^ 2) for i in range(4)])


def load_call(weights, after, name, shares=1):
    n = len(weights)
    shapes = [(w.shape[0], w.shape[1] // shares) for w in weights]
    parts = 4

    def body(*refs):
        sources, targets, sems = refs[:n], refs[n + 1 : 2 * n + 1], refs[-1]
        copies = []
        for i in range(n):
            rows = sources[i].shape[0] // parts
            for j in range(parts):
                span = pl.ds(j * rows, rows)
                copies.append(
                    pltpu.make_async_copy(
                        sources[i].at[span, pl.ds(0, shapes[i][1])], targets[i].at[span], sems.at[i, j]
                    )
                )
        for copy in copies:
            copy.start()
        for copy in copies:
            copy.wait()

    size = sum(w.size * 2 for w in weights) // shares
    return pl.pallas_call(
        body,
        in_specs=[IN_HBM] * n + [pl.BlockSpec(memory_space=pl.ANY)],
        out_specs=[IN_VMEM] * n,
        out_shape=[pltpu.VMEM(shape, w.dtype) for shape, w in zip(shapes, weights)],
        scratch_shapes=[pltpu.SemaphoreType.DMA((n, parts))],
        compiler_params=params(1),
        cost_estimate=cost(0, 2 * size),
        name=name,
    )(*[kept_out(w) for w in weights], after)


def norm_call(tokens, norm_gain, copies, col_width):
    own, features = tokens.shape

    def body(tokens_ref, gain_ref, out_ref, tokens_in, gain_in, scaled, sems):
        loads = [
            pltpu.make_async_copy(tokens_ref, tokens_in, sems.at[0]),
            pltpu.make_async_copy(gain_ref, gain_in, sems.at[1]),
        ]
        for load in loads:
            load.start()
        for load in loads:
            load.wait()
        tokens_f = tokens_in[...].astype(f32)
        squares = jnp.sum(tokens_f * tokens_f, axis=1, keepdims=True)
        scaled[...] = tokens_f * lax.rsqrt(squares / features + epsilon) * gain_in[...]
        first = pl.multiple_of(lax.axis_index("mp") * col_width, col_width)
        mine = scaled[:, pl.ds(first, col_width)].astype(bf16)
        for i in range(copies):
            out_ref[i] = mine

    return pl.pallas_call(
        body,
        in_specs=[IN_HBM] * 2,
        out_specs=IN_VMEM,
        out_shape=jax.ShapeDtypeStruct((copies, own, col_width), bf16),
        scratch_shapes=[
            pltpu.VMEM((own, features), bf16),
            pltpu.VMEM((1, features), f32),
            pltpu.VMEM((own, features), f32),
            pltpu.SemaphoreType.DMA((2,)),
        ],
        compiler_params=params(4),
        cost_estimate=cost(WAIT_FLOPS, 4 * own * features),
        name="norm_rows",
    )(kept_out(tokens), kept_out(norm_gain.reshape(1, features)))


def join_call(blocks):
    n = len(blocks)
    lead = sum(b[0].shape[0] for b in blocks)
    own = blocks[0][0].shape[1]
    cols = [b.shape[2] for b in blocks[0]]
    whole = len(cols) == 1

    def body(*refs):
        a_ref, b_ref = refs[-2:]
        at = 0
        for block, k in zip(blocks, range(0, n * len(cols), len(cols))):
            size = block[0].shape[0]
            if whole:
                half = cols[0] // 2
                a_ref[at : at + size] = refs[k][:, :, :half]
                b_ref[at : at + size] = refs[k][:, :, half:]
            else:
                a_ref[at : at + size] = refs[k][...]
                b_ref[at : at + size] = refs[k + 1][...]
            at += size

    half = cols[0] // 2 if whole else cols[0]
    shape = jax.ShapeDtypeStruct((lead, own, half), bf16)
    flat = [part for block in blocks for part in block]
    return pl.pallas_call(
        body,
        in_specs=[IN_VMEM] * len(flat),
        out_specs=[IN_VMEM] * 2,
        out_shape=[shape, shape],
        compiler_params=params(4),
        cost_estimate=cost(WAIT_FLOPS, 8 * lead * own * half),
        name="join",
    )(*flat)


def order_call(a_blocks, b_blocks, after):
    _, own, half = a_blocks[0].shape

    def body(a0, a1, b0, b1, after_ref, out_ref):
        index = lax.axis_index("dp")
        for refs, order, cols in (
            ((a0, a1), (0, 4, 2, 6, 1, 5, 3, 7), slice(0, half)),
            ((b0, b1), (0, 4, 1, 5, 2, 6, 3, 7), slice(half, 2 * half)),
        ):
            for p, flip in enumerate(order):
                out_ref[lax.bitwise_xor(index, flip), :, cols] = refs[p // 4][p % 4]

    return pl.pallas_call(
        body,
        in_specs=[IN_VMEM] * 4 + [pl.BlockSpec(memory_space=pl.ANY)],
        out_specs=IN_VMEM,
        out_shape=jax.ShapeDtypeStruct((8, own, 2 * half), bf16),
        compiler_params=params(4),
        cost_estimate=cost(0, 64 * own * half),
        name="token_order",
    )(*a_blocks, *b_blocks, after)


def gather_tree(block, v_gate, chunks):
    arrived = swap_dp(block, 4)
    a_two, b_two = join_call([[block], [arrived]])
    a_came, b_came = swap_dp(a_two, 2), swap_dp(b_two, 1)
    a_four, b_four = join_call([[a_two, b_two], [a_came, b_came]])
    a_came, b_came = swap_dp(a_four, 1), swap_dp(b_four, 2)
    (first,) = load_call([v_gate], a_four, "load_first", chunks)
    return order_call((a_four, a_came), (b_four, b_came), held(first)), first


def gate_call(normed, w_gate, w_up, v_gate, chunk, chunks):
    count, depth = normed.shape
    half = count // 2
    width = w_gate.shape[1] // chunks
    block = block_of(width, 256)
    first = chunk * (width // block)

    def body(normed_ref, gate_ref, up_ref, tan_ref, keep_ref, send_ref):
        upper = lax.axis_index("mp") % 2 == 1
        for i, weight in enumerate((gate_ref, up_ref, tan_ref)):
            part = dot(normed_ref[...], weight[...], 1, 0)
            low, high = part[:half], part[half:]
            keep_ref[i] = jnp.where(upper, high, low)
            send_ref[i] = jnp.where(upper, low, high).astype(bf16)

    weight_spec = pl.BlockSpec((depth, block), lambda i: (0, first + i))
    part_spec = pl.BlockSpec((3, half, block), lambda i: (0, 0, i))
    return pl.pallas_call(
        body,
        grid=(width // block,),
        in_specs=[pl.BlockSpec((count, depth), lambda i: (0, 0)), weight_spec, weight_spec, weight_spec],
        out_specs=[part_spec, part_spec],
        out_shape=[
            jax.ShapeDtypeStruct((3, half, width), f32),
            jax.ShapeDtypeStruct((3, half, width), bf16),
        ],
        compiler_params=params(20),
        cost_estimate=cost(6 * count * depth * width, 6 * depth * width),
        name="gate_products",
    )(normed, *[kept_out(w) for w in (w_gate, w_up, v_gate)])


def gate_held_call(normed, w_gate, w_up, v_gate, first_probe, chunk, chunks, after):
    count, depth = normed.shape
    half = count // 2
    width = w_gate.shape[1] // chunks
    block = block_of(width, 512)
    steps = width // block
    first = chunk * width

    def body(normed_ref, gate_ref, up_ref, tan_ref, *rest):
        keep_ref, send_ref, buffer, sems = rest[-4:]
        copies = [
            pltpu.make_async_copy(
                tan_ref.at[:, pl.ds(first + j * block, block)], buffer.at[j], sems.at[j]
            )
            for j in range(0 if chunk == 0 else steps)
        ]
        for copy in copies:
            copy.start()
        upper = lax.axis_index("mp") % 2 == 1
        for i, weight in enumerate((gate_ref, up_ref, None)):
            for j in range(steps):
                span = slice(j * block, (j + 1) * block)
                if weight is None and chunk == 0:
                    right = tan_ref[:, span]
                elif weight is None:
                    copies[j].wait()
                    right = buffer[j]
                else:
                    right = weight[:, first + j * block : first + (j + 1) * block]
                part = dot(normed_ref[...], right, 1, 0)
                low, high = part[:half], part[half:]
                keep_ref[i, :, span] = jnp.where(upper, high, low)
                send_ref[i, :, span] = jnp.where(upper, low, high).astype(bf16)

    probe = held(first_probe) if chunk == 0 else kept_out(v_gate)
    operands = [normed, held(w_gate), held(w_up), probe]
    in_specs = [IN_VMEM] * 3 + [IN_VMEM if chunk == 0 else IN_HBM]
    order(operands, in_specs, after)
    return pl.pallas_call(
        body,
        in_specs=in_specs,
        out_specs=[IN_VMEM] * 2,
        out_shape=[
            jax.ShapeDtypeStruct((3, half, width), f32),
            jax.ShapeDtypeStruct((3, half, width), bf16),
        ],
        scratch_shapes=[
            pltpu.VMEM((steps, depth, block), bf16),
            pltpu.SemaphoreType.DMA((steps,)),
        ],
        compiler_params=params(4 + 2 * depth * width // MIB),
        cost_estimate=cost(6 * count * depth * width, 6 * depth * width),
        name="gate_products",
    )(*operands)


def hidden_call(chip_sum, arrived, after):
    shape = chip_sum.shape[1:]
    width = shape[1]
    block = block_of(width, 512)

    def body(sum_ref, arrived_ref, *rest):
        mine_ref, factor_ref = rest[-2:]
        for j in range(width // block):
            span = slice(j * block, (j + 1) * block)
            gate_pre, up_value, tangent = [
                sum_ref[i, :, span] + arrived_ref[i, :, span].astype(f32) for i in range(3)
            ]
            activation, slope_gate, curvature = silu_parts(gate_pre)
            mine_ref[0, :, span] = (activation * up_value).astype(bf16)
            mine_ref[1, :, span] = (slope_gate * up_value * tangent).astype(bf16)
            factor_ref[0, :, span] = up_value * slope_gate
            factor_ref[1, :, span] = up_value * curvature * tangent

    operands, in_specs = [chip_sum, arrived], [IN_VMEM] * 2
    order(operands, in_specs, after)
    return pl.pallas_call(
        body,
        in_specs=in_specs,
        out_specs=[IN_VMEM] * 2,
        out_shape=[
            jax.ShapeDtypeStruct((2,) + shape, bf16),
            jax.ShapeDtypeStruct((2,) + shape, f32),
        ],
        compiler_params=params(8),
        cost_estimate=cost(0, 30 * shape[0] * width),
        name="hidden_units",
    )(*operands)


def down_call(hiddens, w_down, v_down):
    count = 2 * hiddens[0].shape[1]
    rows, features = w_down.shape
    block = block_of(features, 512)
    n = len(hiddens)

    def body(*refs):
        w_ref, v_ref, out_ref, left = refs[n:]
        join_hidden(refs[:n], left)
        for j in range(features // block):
            span = slice(j * block, (j + 1) * block)
            both = dot(left[...], w_ref[:, span], 1, 0)
            out_ref[0, :, span] = both[:count].astype(bf16)
            out_ref[1, :, span] = (both[count:] + dot(left[:count], v_ref[:, span], 1, 0)).astype(bf16)

    return pl.pallas_call(
        body,
        in_specs=[IN_VMEM] * (n + 2),
        out_specs=IN_VMEM,
        out_shape=jax.ShapeDtypeStruct((2, count, features), bf16),
        scratch_shapes=[pltpu.VMEM((2 * count, rows), bf16)],
        compiler_params=params(12),
        cost_estimate=cost(6 * count * rows * features, 4 * rows * features),
        name="down_products",
    )(*hiddens, held(w_down), held(v_down))


def back_call(residuals, w_down, v_down):
    count, features = residuals.shape[1:]
    half = count // 2
    rows = w_down.shape[0]
    block = block_of(rows, 512)

    def body(res_ref, w_ref, v_ref, keep_ref, send_ref, right):
        right[...] = res_ref[...].reshape(2 * count, features).T
        for j in range(rows // block):
            span = slice(j * block, (j + 1) * block)
            both = dot(w_ref[span, :], right[...], 1, 0)
            tangent = both[:, count:] + dot(v_ref[span, :], right[:, :count], 1, 0)
            for i, part in enumerate((both[:, :count].T, tangent.T)):
                keep_ref[i, :, span] = part[:half]
                send_ref[i, :, span] = part[half:].astype(bf16)

    return pl.pallas_call(
        body,
        in_specs=[IN_VMEM] * 3,
        out_specs=[IN_VMEM] * 2,
        out_shape=[
            jax.ShapeDtypeStruct((2, half, rows), f32),
            jax.ShapeDtypeStruct((2, half, rows), bf16),
        ],
        scratch_shapes=[pltpu.VMEM((features, 2 * count), bf16)],
        compiler_params=params(12),
        cost_estimate=cost(6 * count * rows * features, 4 * rows * features),
        name="back_products",
    )(residuals, held(w_down), held(v_down))


def down_score_call(hiddens, residuals, v_down):
    rows, features = v_down.shape
    count = residuals.shape[1]
    block = block_of(rows, 512)
    steps = rows // block
    n = len(hiddens)

    def body(*refs):
        res_ref, v_ref, out_ref, left, right, buffer, sems = refs[n:]
        join_hidden(refs[:n], left)
        right[:count] = res_ref[1]
        right[count:] = res_ref[0]
        copies = []
        for j in range(steps):
            span = slice(j * block, (j + 1) * block)
            if j >= BUFFERS:
                copies[j - BUFFERS].wait()
            hess = dot(left[:, span], right[...], 0, 0)
            buffer[j % BUFFERS] = (v_ref[span, :].astype(f32) * hess).astype(bf16)
            copies.append(
                pltpu.make_async_copy(
                    buffer.at[j % BUFFERS], out_ref.at[pl.ds(j * block, block)], sems.at[j % BUFFERS]
                )
            )
            copies[j].start()
        for copy in copies[-BUFFERS:]:
            copy.wait()

    return pl.pallas_call(
        body,
        in_specs=[IN_VMEM] * (n + 2),
        out_specs=IN_HBM,
        out_shape=jax.ShapeDtypeStruct((rows, features), bf16),
        scratch_shapes=[
            pltpu.VMEM((2 * count, rows), bf16),
            pltpu.VMEM((2 * count, features), bf16),
            pltpu.VMEM((BUFFERS, block, features), bf16),
            pltpu.SemaphoreType.DMA((BUFFERS,)),
        ],
        compiler_params=params(20),
        cost_estimate=cost(4 * count * rows * features, 4 * rows * features),
        name="down_score",
    )(*hiddens, residuals, held(v_down))


def combine_call(sums, arrived, factors, after):
    n, m = len(sums), len(factors)
    half, part = sums[0].shape[1:]
    width = n * part
    factor_part = factors[0].shape[2]
    block = block_of(math.gcd(part, factor_part), 512)

    def body(*refs):
        sum_refs, arrived_refs, factor_refs = refs[:n], refs[n : 2 * n], refs[2 * n : 2 * n + m]
        out_ref = refs[-1]
        for at in range(0, width, block):
            span = slice(at % part, at % part + block)
            back_grad, back_tangent = [
                sum_refs[at // part][i, :, span] + arrived_refs[at // part][i, :, span].astype(f32)
                for i in range(2)
            ]
            factor_ref = factor_refs[at // factor_part]
            taken = slice(at % factor_part, at % factor_part + block)
            out_ref[:, at : at + block] = (
                back_tangent * factor_ref[0, :, taken] + back_grad * factor_ref[1, :, taken]
            ).astype(bf16)

    return pl.pallas_call(
        body,
        in_specs=[IN_VMEM] * (2 * n + m) + [pl.BlockSpec(memory_space=pl.ANY)],
        out_specs=IN_VMEM,
        out_shape=jax.ShapeDtypeStruct((half, width), bf16),
        compiler_params=params(8),
        cost_estimate=cost(0, 22 * half * width),
        name="combined",
    )(*sums, *arrived, *factors, kept_out(after))


def gate_score_call(normed, combined, v_gate):
    count, depth = normed.shape
    half = count // 2
    width = v_gate.shape[1]
    part = combined[0].shape[1]
    block = block_of(part, 512)
    steps = width // block
    n = len(combined)

    def body(normed_ref, *rest):
        v_ref, out_ref, buffer, sems = rest[n:]
        upper = lax.axis_index("mp") % 2 == 1
        copies = []
        for j in range(steps):
            span = slice(j * block, (j + 1) * block)
            at = j * block // part
            taken = slice(j * block % part, j * block % part + block)
            mine, other = rest[2 * at][:, taken], rest[2 * at + 1][:, taken]
            if j >= BUFFERS:
                copies[j - BUFFERS].wait()
            low = jnp.where(upper, other, mine)
            high = jnp.where(upper, mine, other)
            hess = dot(normed_ref[...], jnp.concatenate([low, high], axis=0), 0, 0)
            buffer[j % BUFFERS] = (v_ref[:, span].astype(f32) * hess).astype(bf16)
            copies.append(
                pltpu.make_async_copy(
                    buffer.at[j % BUFFERS], out_ref.at[:, pl.ds(j * block, block)], sems.at[j % BUFFERS]
                )
            )
            copies[j].start()
        for copy in copies[-BUFFERS:]:
            copy.wait()

    return pl.pallas_call(
        body,
        in_specs=[IN_VMEM] * (n + 2),
        out_specs=IN_HBM,
        out_shape=jax.ShapeDtypeStruct((depth, width), bf16),
        scratch_shapes=[
            pltpu.VMEM((BUFFERS, depth, block), bf16),
            pltpu.SemaphoreType.DMA((BUFFERS,)),
        ],
        compiler_params=params(20),
        cost_estimate=cost(2 * count * depth * width, 4 * depth * width),
        name="gate_score",
    )(normed, *combined, held(v_gate))


def bits():
    index = lax.axis_index("dp")
    return index % 2, (index // 2) % 2


def swap_dp(value, bit):
    return lax.ppermute(value, "dp", [(i, i ^ bit) for i in range(8)])


def piece_call(hiddens, w_down, v_down, away, dtype, groups, after=None):
    count = 2 * hiddens[0].shape[1]
    rows, features = w_down.shape
    n = len(hiddens)
    piece = features // 8

    def body(*refs):
        w_ref, v_ref = refs[n : n + 2]
        out_refs, left = refs[-1 - len(groups) : -1], refs[-1]
        y, z = bits()
        join_hidden(refs[:n], left)
        for out_ref, kind in zip(out_refs, groups):
            base, outer, inner = ((0, y, z), (4, z, y))[kind]
            group = 1 - outer if away else outer
            for k, low in enumerate((1 - inner, inner)):
                first = pl.multiple_of((base + 2 * group + low) * piece, piece)
                both = dot(left[...], w_ref[:, pl.ds(first, piece)], 1, 0)
                tangent = both[count:] + dot(left[:count], v_ref[:, pl.ds(first, piece)], 1, 0)
                out_ref[k, 0] = both[:count].astype(dtype)
                out_ref[k, 1] = tangent.astype(dtype)

    shape = jax.ShapeDtypeStruct((2, 2, count, piece), dtype)
    operands, in_specs = [*hiddens, held(w_down), held(v_down)], [IN_VMEM] * (n + 2)
    order(operands, in_specs, after)
    return pl.pallas_call(
        body,
        in_specs=in_specs,
        out_specs=[IN_VMEM] * len(groups),
        out_shape=[shape] * len(groups),
        scratch_shapes=[pltpu.VMEM((2 * count, rows), bf16)],
        compiler_params=params(8),
        cost_estimate=cost(3 * count * rows * features, 2 * rows * features),
        name="pieces_away" if away else "pieces_home",
    )(*operands)


def residual_call(sums, arrived, target):
    count, features = target.shape
    half = count // 2
    piece = features // 8

    def body(sums_ref, arrived_ref, target_ref, a_ref, b_ref):
        y, z = bits()
        upper = lax.axis_index("mp") % 2 == 1
        for i, (out_ref, outer, inner) in enumerate(((a_ref, y, z), (b_ref, z, y))):
            first = pl.multiple_of((4 * i + 2 * outer + inner) * piece, piece)
            wanted = target_ref[:, pl.ds(first, piece)].astype(f32)
            low, high = wanted[:half], wanted[half:]
            wanted = jnp.concatenate(
                [jnp.where(upper, high, low), jnp.where(upper, low, high)], axis=0
            )
            out_ref[0] = ((sums_ref[i, 0] + arrived_ref[i, 0].astype(f32) - wanted) / count).astype(bf16)
            out_ref[1] = ((sums_ref[i, 1] + arrived_ref[i, 1].astype(f32)) / count).astype(bf16)

    shape = jax.ShapeDtypeStruct((2, count, piece), bf16)
    return pl.pallas_call(
        body,
        in_specs=[IN_VMEM] * 3,
        out_specs=[IN_VMEM] * 2,
        out_shape=[shape, shape],
        compiler_params=params(4),
        cost_estimate=cost(0, 8 * 2 * count * piece),
        name="residuals",
    )(sums, arrived, target)


def back_first_call(a_pieces, b_pieces, w_down, v_down):
    count, piece = a_pieces.shape[2:]
    rows = w_down.shape[0]
    block = block_of(rows, 512)

    def body(a_ref, b_ref, w_ref, v_ref, out_ref, right):
        y, z = bits()
        for i, (ref, inner) in enumerate(((a_ref, z), (b_ref, y))):
            for k, low in enumerate((inner, 1 - inner)):
                first = pl.multiple_of((2 * i + low) * piece, piece)
                right[pl.ds(first, piece), :] = ref[k].reshape(2 * count, piece).T
        starts = [
            pl.multiple_of(2 * piece * y, 2 * piece),
            pl.multiple_of(2 * piece * (2 + z), 2 * piece),
        ]
        for j in range(rows // block):
            span = slice(j * block, (j + 1) * block)
            total = jnp.zeros((block, 2 * count), f32)
            tangent = jnp.zeros((block, count), f32)
            for i, first in enumerate(starts):
                part = right[2 * i * piece : 2 * (i + 1) * piece]
                total += dot(w_ref[span, pl.ds(first, 2 * piece)], part, 1, 0)
                tangent += dot(v_ref[span, pl.ds(first, 2 * piece)], part[:, :count], 1, 0)
            out_ref[span] = jnp.concatenate([total[:, :count], total[:, count:] + tangent], axis=1)

    return pl.pallas_call(
        body,
        in_specs=[IN_VMEM] * 4,
        out_specs=IN_VMEM,
        out_shape=jax.ShapeDtypeStruct((rows, 2 * count), f32),
        scratch_shapes=[pltpu.VMEM((4 * piece, 2 * count), bf16)],
        compiler_params=params(8),
        cost_estimate=cost(12 * count * rows * piece, 8 * rows * piece),
        name="back_first",
    )(a_pieces, b_pieces, held(w_down), held(v_down))


def back_second_call(a_pieces, b_pieces, a_far, b_far, first_part, w_down, v_down, chunk, chunks):
    count, piece = a_pieces.shape[2:]
    half = count // 2
    features = w_down.shape[1]
    rows = w_down.shape[0] // chunks
    block = block_of(rows, 512)
    from_row = chunk * rows

    def body(a_ref, b_ref, a_far_ref, b_far_ref, part_ref, w_ref, v_ref, keep_ref, send_ref, *rest):
        right = rest[-1]
        y, z = bits()
        for i, (ref, far_ref, outer, inner) in enumerate(((a_ref, a_far_ref, y, z), (b_ref, b_far_ref, z, y))):
            for k, low in enumerate((inner, 1 - inner)):
                first = pl.multiple_of((2 * i + low) * piece, piece)
                right[pl.ds(first, piece), :] = far_ref[k].reshape(2 * count, piece).T
                if chunk == 0:
                    near = pl.multiple_of((4 * i + 2 * outer + low) * piece, piece)
                    far = pl.multiple_of((4 * i + 2 * (1 - outer) + low) * piece, piece)
                    for t in range(2):
                        rest[0][t, :, pl.ds(near, piece)] = ref[k, t]
                        rest[0][t, :, pl.ds(far, piece)] = far_ref[k, t]
        starts = [
            pl.multiple_of(2 * piece * (1 - y), 2 * piece),
            pl.multiple_of(2 * piece * (3 - z), 2 * piece),
        ]
        for j in range(rows // block):
            span = slice(j * block, (j + 1) * block)
            taken = slice(from_row + j * block, from_row + (j + 1) * block)
            total = part_ref[taken]
            tangent = jnp.zeros((block, count), f32)
            for i, first in enumerate(starts):
                part = right[2 * i * piece : 2 * (i + 1) * piece]
                total += dot(w_ref[taken, pl.ds(first, 2 * piece)], part, 1, 0)
                tangent += dot(v_ref[taken, pl.ds(first, 2 * piece)], part[:, :count], 1, 0)
            for i, value in enumerate((total[:, :count].T, (total[:, count:] + tangent).T)):
                keep_ref[i, :, span] = value[:half]
                send_ref[i, :, span] = value[half:].astype(bf16)

    out_shape = [
        jax.ShapeDtypeStruct((2, half, rows), f32),
        jax.ShapeDtypeStruct((2, half, rows), bf16),
    ]
    if chunk == 0:
        out_shape.append(jax.ShapeDtypeStruct((2, count, features), bf16))
    return pl.pallas_call(
        body,
        in_specs=[IN_VMEM] * 7,
        out_specs=[IN_VMEM] * len(out_shape),
        out_shape=out_shape,
        scratch_shapes=[pltpu.VMEM((4 * piece, 2 * count), bf16)],
        compiler_params=params(8),
        cost_estimate=cost(12 * count * rows * piece, 8 * rows * piece),
        name="back_second",
    )(a_pieces, b_pieces, a_far, b_far, first_part, held(w_down), held(v_down))


def middle_tree(hiddens, target, w_down, v_down, chunks):
    (a_send,) = piece_call(hiddens, w_down, v_down, True, bf16, (0,))
    (b_send,) = piece_call(hiddens, w_down, v_down, True, bf16, (1,), a_send)
    a_recv, b_recv = swap_dp(a_send, 1), swap_dp(b_send, 2)
    a_home, b_home = piece_call(hiddens, w_down, v_down, False, f32, (0, 1))
    a_sum = a_home + a_recv.astype(f32)
    b_sum = b_home + b_recv.astype(f32)
    a_recv, b_recv = swap_dp(a_sum[0].astype(bf16), 2), swap_dp(b_sum[0].astype(bf16), 1)
    sums = jnp.stack([a_sum[1] + a_recv.astype(f32), b_sum[1] + b_recv.astype(f32)])
    arrived = swap_dp(sums.astype(bf16), 4)
    a_res, b_res = residual_call(sums, arrived, target)
    a_pieces = jnp.stack([a_res, swap_dp(a_res, 2)])
    b_pieces = jnp.stack([b_res, swap_dp(b_res, 1)])
    a_far, b_far = swap_dp(a_pieces, 1), swap_dp(b_pieces, 2)
    first_part = back_first_call(a_pieces, b_pieces, w_down, v_down)
    parts = [
        back_second_call(a_pieces, b_pieces, a_far, b_far, first_part, w_down, v_down, chunk, chunks)
        for chunk in range(chunks)
    ]
    return [chip_sum_of(part[:2]) for part in parts], parts[0][2]


def middle_direct(dp, hiddens, target, w_down, v_down):
    half = hiddens[0].shape[1]
    count = 2 * half
    own = count // dp
    features = w_down.shape[1]
    out_parts = down_call(hiddens, w_down, v_down)
    pieces = out_parts.reshape(2, dp, own, features).swapaxes(0, 1)
    arrived = lax.all_to_all(pieces, "dp", 0, 0, tiled=True).astype(f32)
    totals = jnp.sum(arrived, axis=0)
    core = lax.axis_index("mp") % 2
    first_row = (lax.axis_index("dp") * own + core * half) % count
    target_rows = lax.dynamic_slice_in_dim(target, first_row, own, 0)
    residual_rows = ((totals[0] - target_rows.astype(f32)) / count).astype(bf16)
    residual_tan_rows = (totals[1] / count).astype(bf16)
    rows = jnp.stack([residual_rows, residual_tan_rows])
    spread = lax.all_to_all(
        jnp.broadcast_to(rows[None], (dp,) + rows.shape), "dp", 0, 0, tiled=True
    )
    residuals = spread.swapaxes(0, 1).reshape(2, count, features)
    return [chip_sum_of(back_call(residuals, w_down, v_down))], residuals


def chip_sum_of(product):
    keep, send = product
    chip_sum = keep + swap_core(send).astype(f32)
    return chip_sum, chip_sum.astype(bf16)


def per_device(dp, tokens, norm_gain, target, w_gate, w_up, v_gate, w_down, v_down):
    own = tokens.shape[0]
    count = own * dp
    col_width = w_gate.shape[0]
    chunks, back_chunks = (CHUNKS, BACK_CHUNKS) if dp == 8 else (1, 1)
    if dp == 8:
        block = norm_call(tokens, norm_gain, 1, col_width)
        normed, first = gather_tree(block, v_gate, chunks)
        normed = normed.reshape(count, col_width)
        sums = []
        for chunk in range(chunks):
            after = sums[chunk - 2][1] if chunk > 1 else None
            products = gate_held_call(
                normed, w_gate, w_up, v_gate, first, chunk, chunks, after
            )
            sums.append(chip_sum_of(products))
    else:
        copies = norm_call(tokens, norm_gain, dp, col_width)
        normed = lax.all_to_all(copies, "dp", 0, 0, tiled=True).reshape(count, col_width)
        sums = [chip_sum_of(gate_call(normed, w_gate, w_up, v_gate, 0, 1))]
    arrived = [swap_chip(send) for _, send in sums]
    waits = [None] * chunks
    if dp == 8:
        w_down, v_down = load_call([w_down, v_down], sums[-1][1], "load_down")
        waits = [None] + [w_down] * (chunks - 1)
    hiddens, factors = [], []
    for chunk, ((chip_sum, _), came, wait) in enumerate(zip(sums, arrived, waits)):
        mine, factor = hidden_call(chip_sum, came, None if wait is None else held(wait))
        hiddens += [mine, swap_core(mine)]
        factors.append(factor)
    if dp == 8:
        sums, residuals = middle_tree(hiddens, target, w_down, v_down, back_chunks)
    else:
        sums, residuals = middle_direct(dp, hiddens, target, w_down, v_down)
    arrived = [swap_chip(send) for _, send in sums]
    down_score = down_score_call(hiddens, residuals, v_down)
    mine = combine_call([chip_sum for chip_sum, _ in sums], arrived, factors, down_score)
    combined = [mine, swap_core(mine)]
    gate_score = gate_score_call(normed, combined, v_gate)
    return (gate_score, down_score)


def solution(mesh):
    in_specs = (
        P("dp", None),
        P(),
        P(None, "mp"),
        P("mp", "dp"),
        P("mp", "dp"),
        P("mp", "dp"),
        P("dp", "mp"),
        P("dp", "mp"),
    )
    out_specs = (P("mp", "dp"), P("dp", "mp"))
    return jax.shard_map(
        functools.partial(per_device, mesh.shape["dp"]),
        mesh=mesh,
        in_specs=in_specs,
        out_specs=out_specs,
        check_vma=False,
    )
```
